32 devices in a mesh: section: 2 (over x), wide: 8 (over z, y), tp: 2 (over core).
Axes of the slice: x: 2, y: 2, z: 4, core: 2. Of those that a mesh axis runs over, the one named last changes fastest.
Arguments:
- tokens: bfloat16 [2, 4096, 2048], P(None, ('wide', 'tp')), may hold values from -6 to 6
- out_grad: bfloat16 [2, 4096, 2048], P(None, ('wide', 'tp')), may hold values from -6 to 6
- attn_gain: bfloat16 [2, 2048], P('section', 'wide'), may hold values from 0.25 to 1.75
- w_query: bfloat16 [2, 2048, 2048], P('section', 'wide', 'tp'), may hold values from -0.125 to 0.125
- w_key: bfloat16 [2, 2048, 256], P('section', 'wide', 'tp'), may hold values from -0.125 to 0.125
- w_value: bfloat16 [2, 2048, 256], P('section', 'wide', 'tp'), may hold values from -0.125 to 0.125
- w_out: bfloat16 [2, 2048, 2048], P('section', 'tp', 'wide'), may hold values from -2 to 2
- ffn_gain: bfloat16 [2, 2048], P('section', 'wide'), may hold values from 0.25 to 1.75
- w_gate: bfloat16 [2, 2048, 5632], P('section', 'wide', 'tp'), may hold values from -0.125 to 0.125
- w_up: bfloat16 [2, 2048, 5632], P('section', 'wide', 'tp'), may hold values from -0.125 to 0.125
- w_down: bfloat16 [2, 5632, 2048], P('section', 'tp', 'wide'), may hold values from -0.078125 to 0.078125
Outputs:
- section_out: bfloat16 [2, 2, 4096, 2048], P('section', None, ('wide', 'tp'))
- input_grads: bfloat16 [2, 2, 4096, 2048], P('section', None, ('wide', 'tp'))
- grad_attn_gain: float32 [2, 2048], P('section', 'wide')
- grad_w_query: float32 [2, 2048, 2048], P('section', 'wide', 'tp')
- grad_w_key: float32 [2, 2048, 256], P('section', 'wide', 'tp')
- grad_w_value: float32 [2, 2048, 256], P('section', 'wide', 'tp')
- grad_w_out: float32 [2, 2048, 2048], P('section', 'tp', 'wide')
- grad_ffn_gain: float32 [2, 2048], P('section', 'wide')
- grad_w_gate: float32 [2, 2048, 5632], P('section', 'wide', 'tp')
- grad_w_up: float32 [2, 2048, 5632], P('section', 'wide', 'tp')
- grad_w_down: float32 [2, 5632, 2048], P('section', 'tp', 'wide')
The draws below stay inside these ranges and needn't reach their ends.
All inputs are finite; a program needn't handle non-finite values.
Results may differ from the reference program's by a relative error of at most 0.03.
Values may be sent and summed in bfloat16 or wider, within the bound.
A program may use at most 512 MiB of HBM per device.

```python
import math
import jax
import jax.numpy as jnp
from jax import lax

D = 2048
HQ = 32
KV = 4
HD = 64
FF = 5632
LEN = 4096
MICRO = 2
N_WIDE = 8


def block_levels(own_key, dims, split, smallest, top_value):
    def one(dim, shards_of):
        draws = jax.random.uniform(jax.random.fold_in(jax.random.fold_in(own_key, 6), dim), (shards_of,), jnp.float32, smallest / len(split), top_value / len(split))
        return jnp.repeat(jnp.exp(draws), dims[dim] // shards_of).reshape((-1,) + (1,) * (len(dims) - dim - 1))

    level = one(*split[0])
    for cut in split[1:]:
        level = level * one(*cut)
    return level


def normal_values(key, dims, width, reach, cuts=(), kind=jnp.bfloat16):
    loudness = block_levels(key, dims, cuts, -0.22, 0.18) if cuts else 1.0
    values = jax.random.normal(key, dims, jnp.float32) * width * loudness
    return jnp.minimum(jnp.maximum(values, -reach), reach).astype(kind)


def setup_inputs(seed: int = 0) -> dict:
    streams_of = jax.random.split(jax.random.key(seed), 12)
    tokens = normal_values(streams_of[0], (MICRO, LEN, D), 1.0, 6.0, ((1, 16),))
    out_grad = normal_values(streams_of[1], (MICRO, LEN, D), 1.0, 6.0, ((1, 16),))
    attn_gain = jnp.clip(1.0 + 0.15 * jax.random.normal(streams_of[2], (2, D), jnp.float32), 0.25, 1.75).astype(jnp.bfloat16)
    w_query = normal_values(streams_of[3], (2, D, HQ * HD), D ** -0.5, 0.125, ((0, 2), (1, 8), (2, 2)))
    w_key = normal_values(streams_of[4], (2, D, KV * HD), D ** -0.5, 0.125, ((0, 2), (1, 8), (2, 2)))
    w_value = normal_values(streams_of[5], (2, D, KV * HD), D ** -0.5, 0.125, ((0, 2), (1, 8), (2, 2)))
    w_out = normal_values(streams_of[6], (2, HQ * HD, D), (max(1, HQ * HD * 16 // LEN)) ** -0.5, 2.0, ((0, 2), (1, 2), (2, 8)))
    ffn_gain = jnp.clip(1.0 + 0.15 * jax.random.normal(streams_of[7], (2, D), jnp.float32), 0.25, 1.75).astype(jnp.bfloat16)
    w_gate = normal_values(streams_of[8], (2, D, FF), D ** -0.5, 0.125, ((0, 2), (1, 8), (2, 2)))
    w_up = normal_values(streams_of[9], (2, D, FF), D ** -0.5, 0.125, ((0, 2), (1, 8), (2, 2)))
    w_down = normal_values(streams_of[10], (2, FF, D), FF ** -0.5, 0.078125, ((0, 2), (1, 2), (2, 8)))
    return dict(tokens=tokens, out_grad=out_grad, attn_gain=attn_gain, w_query=w_query, w_key=w_key, w_value=w_value, w_out=w_out, ffn_gain=ffn_gain, w_gate=w_gate, w_up=w_up, w_down=w_down)


@jax.custom_vjp
def low(v):
    return lax.optimization_barrier(v.astype(jnp.bfloat16)).astype(jnp.float32)

@jax.custom_vjp
def low_back(v):
    return v

def low_keep(v):
    return (low(v), None)

def low_pass(kept, grad):
    return (grad,)

def back_keep(v):
    return (v, None)

def back_low(kept, grad):
    return (low(grad),)
low.defvjp(low_keep, low_pass)
low_back.defvjp(back_keep, back_low)

def product(left, right):
    return jnp.dot(left, right, precision=lax.Precision.HIGHEST, preferred_element_type=jnp.float32)

def rope_tables(length):
    inverse = 1.0 / 10000.0 ** (jnp.arange(0, HD, 2).astype(jnp.float32) / HD)
    angle = jnp.arange(length).astype(jnp.float32)[:, None] * inverse[None, :]
    return (jnp.cos(angle), jnp.sin(angle))

def rotate(heads, cosine, sine_part):
    half = heads.shape[-1] // 2
    first = heads[..., :half]
    second = heads[..., half:]
    cos_rows = cosine[:, None, :]
    sin_rows = sine_part[:, None, :]
    return jnp.concatenate([first * cos_rows - second * sin_rows, second * cos_rows + first * sin_rows], axis=-1)

def rms_norm(values, gain):
    return values * lax.rsqrt(lax.optimization_barrier(jnp.mean(values * values, axis=-1, keepdims=True)) + 1e-05) * gain

def section_layer(inputs, attn_gain, w_query, w_key, w_value, w_out, ffn_gain, w_gate, w_up, w_down):
    length = inputs.shape[0]
    group = HQ // KV
    block_rows = length // N_WIDE
    softmax_scale = 1.0 / math.sqrt(HD)
    normed = low(rms_norm(inputs, attn_gain))
    cosine, sine_part = rope_tables(length)
    queries = low(rotate(low_back(product(normed, w_query)).reshape(length, HQ, HD), cosine, sine_part))
    keys_all = low(rotate(low_back(product(normed, w_key)).reshape(length, KV, HD), cosine, sine_part))
    values_all = low(low_back(product(normed, w_value))).reshape(length, KV, HD)
    query_blocks = queries.reshape(N_WIDE, block_rows, KV, group, HD)
    block_starts = (jnp.arange(N_WIDE) * block_rows).astype(jnp.int32)
    key_places = jnp.arange(length).astype(jnp.int32)

    def per_block(operands):
        query_block, start = operands
        scores = low_back(jnp.einsum('qkgd,tkd->kgqt', query_block, keys_all, precision=lax.Precision.HIGHEST)) * softmax_scale
        query_places = start + jnp.arange(block_rows).astype(jnp.int32)
        visible = key_places[None, :] <= query_places[:, None]
        scores = jnp.where(visible, scores, -1e+30)
        probs = low(jax.nn.softmax(scores, axis=-1))
        return jnp.einsum('kgqt,tkd->qkgd', probs, values_all, precision=lax.Precision.HIGHEST)
    attended = lax.map(jax.checkpoint(per_block), (query_blocks, block_starts))
    attended = low(low_back(attended.reshape(length, HQ * HD)))
    middle = inputs + low_back(product(attended, w_out))
    normed_ffn = low(rms_norm(middle, ffn_gain))
    gate_pre = low_back(product(normed_ffn, w_gate))
    up_proj = low_back(product(normed_ffn, w_up))
    hidden = low(jax.nn.silu(gate_pre) * up_proj)
    return middle + low_back(product(hidden, w_down))

def sectioned(inputs, *weights):
    return low(low_back(section_layer(inputs, *weights)))

def reference(tokens, out_grad, attn_gain, w_query, w_key, w_value, w_out, ffn_gain, w_gate, w_up, w_down):
    params = [item.astype(jnp.float32) for item in (attn_gain, w_query, w_key, w_value, w_out, ffn_gain, w_gate, w_up, w_down)]
    first_weights = [item[0] for item in params]
    second_weights = [item[1] for item in params]
    first_sums = [jnp.zeros_like(item) for item in first_weights]
    second_sums = [jnp.zeros_like(item) for item in second_weights]
    first_outs = []
    second_outs = []
    first_grads = []
    second_grads = []
    for micro_slot in range(MICRO):
        first_result, first_back = jax.vjp(sectioned, tokens[micro_slot].astype(jnp.float32), *first_weights)
        second_result, second_back = jax.vjp(sectioned, first_result, *second_weights)
        second_cot = second_back(out_grad[micro_slot].astype(jnp.float32))
        first_cot = first_back(second_cot[0])
        second_sums = [total + extra for total, extra in zip(second_sums, second_cot[1:])]
        first_sums = [total + extra for total, extra in zip(first_sums, first_cot[1:])]
        first_outs.append(first_result)
        second_outs.append(second_result)
        first_grads.append(first_cot[0])
        second_grads.append(second_cot[0])
    section_out = jnp.stack([jnp.stack(first_outs), jnp.stack(second_outs)]).astype(jnp.bfloat16)
    input_grads = jnp.stack([jnp.stack(first_grads), jnp.stack(second_grads)]).astype(jnp.bfloat16)
    stacked = [jnp.stack([first, second]) for first, second in zip(first_sums, second_sums)]
    return (section_out, input_grads, stacked[0], stacked[1], stacked[2], stacked[3], stacked[4], stacked[5], stacked[6], stacked[7], stacked[8])
```

```python
import functools
import math

import jax
import jax.numpy as jnp
from jax import lax
from jax.experimental import pallas as pl
from jax.experimental.pallas import tpu as pltpu
from jax.sharding import PartitionSpec as P

HD = 64
PAIR = 2 * HD
EPSILON = 1e-05
GAIN_ROWS = 16
VMEM = 48 * 2**20
BF = jnp.bfloat16
F32 = jnp.float32
ANY = pl.BlockSpec(memory_space=pl.ANY)


def partner(x, axis, bit):
    peers = lax.axis_size(axis)
    return lax.ppermute(x, axis, [(i, i ^ bit) for i in range(peers)])


def after(value, *events):
    return lax.optimization_barrier((value,) + events)[0]


def product(left, right):
    return jnp.dot(left, right, preferred_element_type=F32)


def cross(left, right):
    return lax.dot_general(left, right, (((0,), (0,)), ((), ())), preferred_element_type=F32)


def against(left, right):
    return lax.dot_general(left, right, (((1,), (1,)), ((), ())), preferred_element_type=F32)


def call(body, ins, outs, scratch, flops, exps=0, **more):
    moved = sum(x.size * x.dtype.itemsize for x in list(ins) + list(outs))
    return pl.pallas_call(
        body,
        out_shape=outs,
        scratch_shapes=scratch,
        compiler_params=pltpu.CompilerParams(vmem_limit_bytes=VMEM),
        cost_estimate=pl.CostEstimate(
            flops=int(flops), bytes_accessed=int(moved), transcendentals=int(exps)
        ),
        **more,
    )(*ins)


def shaped(*dims, kind=BF):
    return jax.ShapeDtypeStruct(dims, kind)


def lines():
    count = lax.axis_size("wide")
    return [list(range(y, count, 2)) for y in range(2)]


def side():
    return lax.axis_index("wide") % 2


def gather_line(shard):
    return lax.all_gather(shard, "wide", axis=0, tiled=True, axis_index_groups=lines())


def reduce_line(near):
    return lax.psum_scatter(
        near, "wide", scatter_dimension=0, tiled=True, axis_index_groups=lines()
    )


def gather_blocks(shard):
    count = lax.axis_size("wide")
    far = [shard if k == 0 else partner(shard, "wide", k) for k in range(0, count, 2)]
    blocks = []
    for block in far:
        blocks += [block, partner(block, "wide", 1)]
    return blocks


def reduce_blocks(send, keep):
    near = keep.astype(F32) + partner(send, "wide", 1).astype(F32)
    total = near[0]
    for j in range(1, keep.shape[0]):
        total = total + partner(near[j].astype(BF), "wide", 2 * j).astype(F32)
    return total


def mirror(x):
    count = lax.axis_size("wide")
    pairs = []
    for w in range(count):
        pairs.append((2 * w, 2 * w))
        pairs.append((2 * w + 1, 2 * (count - 1 - w) + 1))
    return lax.ppermute(x, ("wide", "tp"), pairs)


def spread(values):
    other = partner(values, "section", 1)
    return [values, other, partner(values, "tp", 1), partner(other, "tp", 1)]


def fold(own, send):
    rows = own.shape[0] // 2
    got = partner(send, "tp", 1)
    away = (own[rows:].astype(F32) + got[rows:].astype(F32)).astype(BF)
    mine = own[:rows].astype(F32) + got[:rows].astype(F32)
    return mine + partner(away, "section", 1).astype(F32)


def load_attn(ref, dest, sem, depth, start):
    copies = []
    for k in range(dest.shape[0] // depth):
        copies.append(
            pltpu.make_async_copy(
                ref.at[pl.ds(k * (depth + GAIN_ROWS), depth), pl.ds(start, dest.shape[1])],
                dest.at[pl.ds(k * depth, depth)],
                sem.at[k],
            )
        )
        copies[-1].start()
    return copies


def load_sides(refs, dest, sem, depth, first=0):
    copies = []
    y = side()
    for s, ref in enumerate(refs):
        for j in range(dest.shape[0] // (2 * depth)):
            place = pl.multiple_of((2 * j + (y + s) % 2) * depth, depth)
            copies.append(
                pltpu.make_async_copy(
                    ref.at[pl.ds(j * depth, depth)],
                    dest.at[pl.ds(place, depth)],
                    sem.at[first + 2 * j + s],
                )
            )
            copies[-1].start()
    return copies


def qkv_kernel(depth, *refs):
    pieces, attn, tables = refs[:4], refs[4], refs[5:9]
    q_ref, kv_ref, w, sem = refs[9:]
    width = w.shape[1]
    for copy in load_attn(attn, w, sem, depth, 0):
        copy.wait()
    cos, sin, cos_kv, sin_kv = tables
    for p, piece in enumerate(pieces):
        linear = product(piece[...], w[...])
        micro, rows = q_ref.shape[1], q_ref.shape[2]
        first = lax.broadcasted_iota(jnp.int32, (rows, PAIR), 1) % HD < HD // 2
        span = slice(p * rows, (p + 1) * rows)
        for m in range(micro):
            for start in range(0, width, PAIR):
                part = linear[m * rows : (m + 1) * rows, start : start + PAIR]
                turned = jnp.where(
                    first, pltpu.roll(part, PAIR - HD // 2, 1), pltpu.roll(part, HD // 2, 1)
                )
                if start + PAIR < width:
                    out = part * cos[span] + turned * sin[span]
                    q_ref[p, m, :, start : start + PAIR] = out.astype(BF)
                else:
                    out = part * cos_kv[span] + turned * sin_kv[span]
                    kv_ref[p, m] = out.astype(BF)


def qkv_project(pieces, attn, tables, micro, depth, width):
    total, d = pieces[0].shape
    rows = total // micro
    vmem = pl.BlockSpec(memory_space=pltpu.VMEM)
    return call(
        functools.partial(qkv_kernel, depth),
        [*pieces, attn, *tables],
        [shaped(4, micro, rows, width - PAIR), shaped(4, micro, rows, PAIR)],
        [pltpu.VMEM((d, width), BF), pltpu.SemaphoreType.DMA((d // depth,))],
        8 * total * d * width,
        in_specs=[vmem] * 4 + [ANY] + [vmem] * 4,
        out_specs=[vmem] * 2,
    )


def gate_up_kernel(depth, *refs):
    pieces, gates, ups = refs[:4], refs[4:6], refs[6:8]
    outs = refs[8:11]
    x, w_gate, w_up, buffer, x_sem, w_sem, out_sem = refs[11:]
    copies = load_sides(gates, w_gate, w_sem, depth)
    copies += load_sides(ups, w_up, w_sem, depth, w_gate.shape[0] // depth)
    inputs = []
    for p, piece in enumerate(pieces):
        inputs.append(pltpu.make_async_copy(piece, x.at[p], x_sem.at[p]))
        inputs[-1].start()
    for copy in copies:
        copy.wait()
    rows = x.shape[1]
    results = []
    for p in range(4):
        inputs[p].wait()
        gate = product(x[p], w_gate[...])
        up = product(x[p], w_up[...])
        if p >= 2:
            for copy in results[p - 2]:
                copy.wait()
        slot = p % 2
        buffer[slot, 0] = gate.astype(BF)
        buffer[slot, 1] = up.astype(BF)
        buffer[slot, 2] = (gate * jax.nn.sigmoid(gate) * up).astype(BF)
        results.append(
            [
                pltpu.make_async_copy(
                    buffer.at[slot, i], outs[i].at[pl.ds(p * rows, rows)], out_sem.at[p, i]
                )
                for i in range(3)
            ]
        )
        for copy in results[p]:
            copy.start()
    for p in (2, 3):
        for copy in results[p]:
            copy.wait()


def gate_up(pieces, gates, ups, depth):
    rows, d = pieces[0].shape
    hidden = gates[0].shape[1]
    return call(
        functools.partial(gate_up_kernel, depth),
        [*pieces, *gates, *ups],
        [shaped(4 * rows, hidden)] * 3,
        [
            pltpu.VMEM((4, rows, d), BF),
            pltpu.VMEM((d, hidden), BF),
            pltpu.VMEM((d, hidden), BF),
            pltpu.VMEM((2, 3, rows, hidden), BF),
            pltpu.SemaphoreType.DMA((4,)),
            pltpu.SemaphoreType.DMA((2 * d // depth,)),
            pltpu.SemaphoreType.DMA((4, 3)),
        ],
        16 * rows * d * hidden,
        4 * rows * hidden,
        in_specs=[ANY] * 8,
        out_specs=[ANY] * 3,
    )


def hidden_back_kernel(depth, *refs):
    pieces, downs = refs[:4], refs[4:6]
    gate_ref, up_ref = refs[6:8]
    outs = refs[8:10]
    x, w, kept, buffer, x_sem, w_sem, kept_sem, out_sem = refs[10:]
    copies = load_sides(downs, w, w_sem, depth)
    rows = x.shape[1]
    inputs = []
    for p, piece in enumerate(pieces):
        span = pl.ds(p * rows, rows)
        inputs.append(
            [
                pltpu.make_async_copy(piece, x.at[p], x_sem.at[p]),
                pltpu.make_async_copy(gate_ref.at[span], kept.at[p, 0], kept_sem.at[p, 0]),
                pltpu.make_async_copy(up_ref.at[span], kept.at[p, 1], kept_sem.at[p, 1]),
            ]
        )
        for copy in inputs[-1]:
            copy.start()
    for copy in copies:
        copy.wait()
    results = []
    for p in range(4):
        for copy in inputs[p]:
            copy.wait()
        grad = product(x[p], w[...])
        gate = kept[p, 0].astype(F32)
        up = kept[p, 1].astype(F32)
        sigma = jax.nn.sigmoid(gate)
        if p >= 2:
            for copy in results[p - 2]:
                copy.wait()
        slot = p % 2
        buffer[slot, 0] = (grad * up * sigma * (1.0 + gate * (1.0 - sigma))).astype(BF)
        buffer[slot, 1] = (grad * gate * sigma).astype(BF)
        results.append(
            [
                pltpu.make_async_copy(
                    buffer.at[slot, i], outs[i].at[pl.ds(p * rows, rows)], out_sem.at[p, i]
                )
                for i in range(2)
            ]
        )
        for copy in results[p]:
            copy.start()
    for p in (2, 3):
        for copy in results[p]:
            copy.wait()


def hidden_back(pieces, downs, gate, up, depth):
    rows, d = pieces[0].shape
    hidden = downs[0].shape[1]
    return call(
        functools.partial(hidden_back_kernel, depth),
        [*pieces, *downs, gate, up],
        [shaped(4 * rows, hidden)] * 2,
        [
            pltpu.VMEM((4, rows, d), BF),
            pltpu.VMEM((d, hidden), BF),
            pltpu.VMEM((4, 2, rows, hidden), BF),
            pltpu.VMEM((2, 2, rows, hidden), BF),
            pltpu.SemaphoreType.DMA((4,)),
            pltpu.SemaphoreType.DMA((d // depth,)),
            pltpu.SemaphoreType.DMA((4, 2)),
            pltpu.SemaphoreType.DMA((4, 2)),
        ],
        8 * rows * d * hidden,
        4 * rows * hidden,
        in_specs=[ANY] * 8,
        out_specs=[ANY] * 2,
    )


def out_back_kernel(depth, offset, *refs):
    pieces, attn = refs[:4], refs[4]
    out_ref, w, sem = refs[5:]
    for copy in load_attn(attn, w, sem, depth, offset):
        copy.wait()
    rows = pieces[0].shape[0]
    for p, piece in enumerate(pieces):
        out_ref[p * rows : (p + 1) * rows] = product(piece[...], w[...]).astype(BF)


def out_back(pieces, attn, depth, offset, width):
    rows, d = pieces[0].shape
    vmem = pl.BlockSpec(memory_space=pltpu.VMEM)
    return call(
        functools.partial(out_back_kernel, depth, offset),
        [*pieces, attn],
        [shaped(4 * rows, width)],
        [pltpu.VMEM((d, width), BF), pltpu.SemaphoreType.DMA((d // depth,))],
        8 * rows * d * width,
        in_specs=[vmem] * 4 + [ANY],
        out_specs=[vmem],
    )[0]


def contract_kernel(depth, starts, *refs):
    sides = len(starts)
    lefts, refs = refs[:sides], refs[sides:]
    sources = []
    for start in starts:
        size = 2 if start is None else 1
        sources.append(refs[:size])
        refs = refs[size:]
    own_ref, send_ref = refs[:2]
    weights, sem = refs[2:-1], refs[-1]
    step = pl.program_id(0)
    half = pl.num_programs(0) // 2

    @pl.when(step == 0)
    def _():
        copies = []
        for s, start in enumerate(starts):
            if start is None:
                copies += load_sides(sources[s], weights[s], sem.at[s], depth)
            else:
                copies += load_attn(sources[s][0], weights[s], sem.at[s], depth, start)
        for copy in copies:
            copy.wait()

    total = against(lefts[0][...], weights[0][...])
    for s in range(1, sides):
        total = total + against(lefts[s][...], weights[s][...])
    total = total.astype(BF)

    @pl.when(step < half)
    def _():
        send_ref[...] = total

    @pl.when(step >= half)
    def _():
        own_ref[...] = total


def contract(lefts, sources, starts, depth, width):
    sides = len(lefts)
    total = lefts[0].shape[0]
    tile = total // 4
    flat = [ref for group in sources for ref in group]
    return call(
        functools.partial(contract_kernel, depth, starts),
        [*lefts, *flat],
        [shaped(total // 2, width)] * 2,
        [pltpu.VMEM((width, left.shape[1]), BF) for left in lefts]
        + [pltpu.SemaphoreType.DMA((sides, width // depth))],
        sum(2 * total * left.shape[1] * width for left in lefts),
        grid=(4,),
        in_specs=[
            pl.BlockSpec((tile, left.shape[1]), lambda i: ((i + 2) % 4, 0)) for left in lefts
        ]
        + [ANY] * len(flat),
        out_specs=[
            pl.BlockSpec((tile, width), lambda i: (jnp.maximum(i - 2, 0), 0)),
            pl.BlockSpec((tile, width), lambda i: (jnp.minimum(i, 1), 0)),
        ],
    )


def weight_kernel(x0, x1, x2, x3, right_ref, send_ref, keep_ref):
    left = jnp.concatenate([x0[...], x1[...], x2[...], x3[...]], axis=0)
    grad = cross(left, right_ref[...]).astype(BF)
    depth = keep_ref.shape[1]
    for y, (first, second) in enumerate(((keep_ref, send_ref), (send_ref, keep_ref))):

        @pl.when(side() == y)
        def _():
            first[0] = grad[:depth]
            second[0] = grad[depth:]


def weight_grad(pieces, right, n):
    rows, d = pieces[0].shape
    width = right.shape[1]
    depth = d // n
    out = pl.BlockSpec((1, depth, width), lambda j: (j, 0, 0))
    return call(
        weight_kernel,
        [*pieces, right],
        [shaped(n // 2, depth, width)] * 2,
        [],
        8 * rows * d * width,
        grid=(n // 2,),
        in_specs=[pl.BlockSpec((rows, 2 * depth), lambda j: (0, j))] * 4
        + [pl.BlockSpec((4 * rows, width), lambda j: (0, 0))],
        out_specs=[out, out],
    )


def attn_weight_kernel(*refs):
    xs, gs = refs[:4], refs[4:8]
    dq_ref, dkv_ref, att_ref, gain_ref, send_ref, keep_ref = refs[8:]
    depth = keep_ref.shape[1] - GAIN_ROWS
    left = jnp.concatenate([x[...] for x in xs], axis=0)
    grad = jnp.concatenate([g[...] for g in gs], axis=0)
    start = 0
    for source, right in ((left, dq_ref), (left, dkv_ref), (grad, att_ref)):
        term = cross(source, right[...]).astype(BF)
        span = slice(start, start + right.shape[1])
        start += right.shape[1]
        for y, (first, second) in enumerate(((keep_ref, send_ref), (send_ref, keep_ref))):

            @pl.when(side() == y)
            def _():
                first[0, :depth, span] = term[:depth]
                second[0, :depth, span] = term[depth:]

    for y, (first, second) in enumerate(((keep_ref, send_ref), (send_ref, keep_ref))):

        @pl.when(side() == y)
        def _():
            first[0, depth:] = gain_ref[0, 0]
            second[0, depth:] = gain_ref[0, 1]


def attn_weight_grad(xs, gs, dq, dkv, attended, gains, n):
    rows, d = xs[0].shape
    depth = d // n
    width = dq.shape[1] + dkv.shape[1] + attended.shape[1]
    out = pl.BlockSpec((1, depth + GAIN_ROWS, width), lambda j: (j, 0, 0))
    whole = lambda x: pl.BlockSpec(x.shape, lambda j: (0, 0))
    return call(
        attn_weight_kernel,
        [*xs, *gs, dq, dkv, attended, gains],
        [shaped(n // 2, depth + GAIN_ROWS, width)] * 2,
        [],
        8 * rows * d * width,
        grid=(n // 2,),
        in_specs=[pl.BlockSpec((rows, 2 * depth), lambda j: (0, j))] * 8
        + [
            whole(dq),
            whole(dkv),
            whole(attended),
            pl.BlockSpec((1, 2, GAIN_ROWS, width), lambda j: (j, 0, 0, 0)),
        ],
        out_specs=[out, out],
    )


def stack_heads(x):
    return jnp.concatenate([x[:, h : h + HD] for h in range(0, x.shape[1], HD)], axis=0)


def turn_heads(x):
    pairs = [x[:, g : g + PAIR].T for g in range(0, x.shape[1], PAIR)]
    return jnp.concatenate([part for pair in pairs for part in (pair[:HD], pair[HD:])], axis=1)


def back_heads(x, rows, g):
    even = x[:, 2 * g * rows : (2 * g + 1) * rows]
    odd = x[:, (2 * g + 1) * rows : (2 * g + 2) * rows]
    return jnp.concatenate([even, odd], axis=0).T


def attend_kernel(
    block, loc_ref, pos_ref, q_ref, kv_ref, o_ref, lse_ref, k_ref, vt_ref, m_ref, acc_ref
):
    piece = pl.program_id(1)
    rows = q_ref.shape[2]
    count = kv_ref.shape[0]
    per_block = block // rows

    @pl.when(piece == 0)
    def _():
        def one(i, _):
            kv = kv_ref[loc_ref[i], 0]
            k_ref[i] = kv[:, :HD]
            ones = jnp.ones((GAIN_ROWS, rows), BF)
            vt_ref[i] = jnp.concatenate([kv.T[HD:], ones], axis=0)
            return 0

        lax.fori_loop(0, count, one, 0)

    pos = pos_ref[piece]
    queries = turn_heads(q_ref[0, 0] * BF(1.0 / math.sqrt(HD)))
    m_ref[...] = jnp.full(m_ref.shape, -1e30, F32)
    acc_ref[...] = jnp.zeros(acc_ref.shape, F32)

    def step(j, masked):
        first = j * per_block
        keys = jnp.concatenate([k_ref[first + i] for i in range(per_block)], axis=0)
        values = jnp.concatenate([vt_ref[first + i] for i in range(per_block)], axis=1)
        scores = product(keys, queries)
        if masked:
            row = lax.broadcasted_iota(jnp.int32, scores.shape, 0)
            column = lax.broadcasted_iota(jnp.int32, scores.shape, 1) % rows
            scores = jnp.where(row + j * block <= column + pos, scores, -1e30)
        before = m_ref[...]
        now = jnp.maximum(before, jnp.max(scores, axis=0, keepdims=True))
        terms = jnp.exp(scores - now)
        shrink = jnp.exp(before - now)
        acc_ref[...] = acc_ref[...] * shrink + product(values, terms.astype(BF))
        m_ref[...] = now

    full = pos // block

    def loop(j, _):
        step(j, False)
        return 0

    lax.fori_loop(0, full, loop, 0)
    step(full, True)
    total = acc_ref[HD : HD + 1]
    out = acc_ref[:HD] / total
    lse_ref[0, 0] = m_ref[...] + jnp.log(total)
    for g in range(q_ref.shape[3] // PAIR):
        o_ref[0, 0, :, g * PAIR : (g + 1) * PAIR] = back_heads(out, rows, g).astype(BF)


def attend(q, kv, loc, pos):
    pieces, micro, rows, width = q.shape
    count = kv.shape[0]
    stacked = rows * width // HD
    block = min(512, rows * count)
    scores = micro * pieces * stacked * rows * count // 2
    heads = pl.BlockSpec((1, 1, rows, width), lambda m, p, *_: (p, m, 0, 0))
    return call(
        functools.partial(attend_kernel, block),
        [loc, pos, q, kv],
        [shaped(*q.shape), shaped(pieces, micro, 1, stacked, kind=F32)],
        (),
        scores * 2750,
        scores,
        grid_spec=pltpu.PrefetchScalarGridSpec(
            num_scalar_prefetch=2,
            grid=(micro, pieces),
            in_specs=[
                heads,
                pl.BlockSpec((count, 1, rows, PAIR), lambda m, p, *_: (0, m, 0, 0)),
            ],
            out_specs=[
                heads,
                pl.BlockSpec((1, 1, 1, stacked), lambda m, p, *_: (p, m, 0, 0)),
            ],
            scratch_shapes=[
                pltpu.VMEM((count, rows, HD), BF),
                pltpu.VMEM((count, HD + GAIN_ROWS, rows), BF),
                pltpu.VMEM((1, stacked), F32),
                pltpu.VMEM((HD + GAIN_ROWS, stacked), F32),
            ],
        ),
    )


def attend_back_kernel(
    block,
    loc_ref,
    pos_ref,
    q_ref,
    do_ref,
    o_ref,
    lse_ref,
    kv_ref,
    cos_ref,
    sin_ref,
    dq_ref,
    send_ref,
    keep_ref,
    k_ref,
    v_ref,
    kt_ref,
    dq_acc,
    dk_acc,
    dv_acc,
):
    piece = pl.program_id(1)
    rows = q_ref.shape[2]
    count = kv_ref.shape[0]
    per_block = block // rows
    scale = 1.0 / math.sqrt(HD)

    @pl.when(piece == 0)
    def _():
        def one(i, _):
            kv = kv_ref[loc_ref[i], 0]
            k_ref[i] = kv[:, :HD]
            v_ref[i] = kv[:, HD:]
            kt_ref[i] = kv.T[:HD]
            dk_acc[i] = jnp.zeros(dk_acc.shape[1:], F32)
            dv_acc[i] = jnp.zeros(dv_acc.shape[1:], F32)
            return 0

        lax.fori_loop(0, count, one, 0)

    pos = pos_ref[piece]
    q = q_ref[0, 0] * BF(scale)
    do = do_ref[0, 0]
    queries, queries_t = stack_heads(q), turn_heads(q)
    grads, grads_t = stack_heads(do), turn_heads(do)
    dots = turn_heads(do.astype(F32) * o_ref[0, 0].astype(F32))
    delta = jnp.sum(dots, axis=0, keepdims=True)
    logs = lse_ref[0, 0]
    dq_acc[...] = jnp.zeros(dq_acc.shape, F32)

    def step(j, masked):
        first = j * per_block
        keys = jnp.concatenate([k_ref[first + i] for i in range(per_block)], axis=0)
        values = jnp.concatenate([v_ref[first + i] for i in range(per_block)], axis=0)
        keys_t = jnp.concatenate([kt_ref[first + i] for i in range(per_block)], axis=1)
        scores = product(keys, queries_t)
        probs = jnp.exp(scores - logs)
        if masked:
            row = lax.broadcasted_iota(jnp.int32, scores.shape, 0)
            column = lax.broadcasted_iota(jnp.int32, scores.shape, 1) % rows
            probs = jnp.where(row + j * block <= column + pos, probs, 0.0)
        grad_probs = product(values, grads_t)
        grad_low = (probs * (grad_probs - delta)).astype(BF)
        dv = product(probs.astype(BF), grads)
        dk = product(grad_low, queries)
        dq_acc[...] += product(keys_t, grad_low)
        for i in range(per_block):
            dk_acc[first + i] += dk[i * rows : (i + 1) * rows]
            dv_acc[first + i] += dv[i * rows : (i + 1) * rows]

    full = pos // block

    def loop(j, _):
        step(j, False)
        return 0

    lax.fori_loop(0, full, loop, 0)
    step(full, True)

    first = lax.broadcasted_iota(jnp.int32, (rows, PAIR), 1) % HD < HD // 2
    for g in range(q_ref.shape[3] // PAIR):
        part = back_heads(dq_acc[...], rows, g) * scale
        turned = jnp.where(
            first, pltpu.roll(part, PAIR - HD // 2, 1), pltpu.roll(part, HD // 2, 1)
        )
        out = part * cos_ref[...] - turned * sin_ref[...]
        dq_ref[0, 0, :, g * PAIR : (g + 1) * PAIR] = out.astype(BF)

    @pl.when(piece == pl.num_programs(1) - 1)
    def _():
        pieces = pl.num_programs(1)

        def one(i, _):
            grad = jnp.concatenate([dk_acc[i], dv_acc[i]], axis=1).astype(BF)
            place = loc_ref[i]
            owner = place // pieces
            slot = owner // 2 * pieces + place % pieces

            @pl.when(owner % 2 == 0)
            def _():
                keep_ref[slot, 0] = grad

            @pl.when(owner % 2 == 1)
            def _():
                send_ref[slot, 0] = grad

            return 0

        lax.fori_loop(0, count, one, 0)


def attend_back(q, grad, attended, lse, kv, cos, sin, loc, pos):
    pieces, micro, rows, width = q.shape
    count = kv.shape[0]
    stacked = rows * width // HD
    block = min(512, rows * count)
    scores = micro * pieces * stacked * rows * count // 2
    heads = pl.BlockSpec((1, 1, rows, width), lambda m, p, *_: (p, m, 0, 0))
    whole = pl.BlockSpec((count, 1, rows, PAIR), lambda m, p, *_: (0, m, 0, 0))
    half = pl.BlockSpec((count // 2, 1, rows, PAIR), lambda m, p, *_: (0, m, 0, 0))
    table = pl.BlockSpec((rows, PAIR), lambda m, p, *_: (p, 0))
    return call(
        functools.partial(attend_back_kernel, block),
        [loc, pos, q, grad, attended, lse, kv, cos, sin],
        [shaped(*q.shape)] + [shaped(count // 2, micro, rows, PAIR)] * 2,
        (),
        scores * 4600,
        scores,
        grid_spec=pltpu.PrefetchScalarGridSpec(
            num_scalar_prefetch=2,
            grid=(micro, pieces),
            in_specs=[
                heads,
                heads,
                heads,
                pl.BlockSpec((1, 1, 1, stacked), lambda m, p, *_: (p, m, 0, 0)),
                whole,
                table,
                table,
            ],
            out_specs=[heads, half, half],
            scratch_shapes=[
                pltpu.VMEM((count, rows, HD), BF),
                pltpu.VMEM((count, rows, HD), BF),
                pltpu.VMEM((count, HD, rows), BF),
                pltpu.VMEM((HD, stacked), F32),
                pltpu.VMEM((count, rows, HD), F32),
                pltpu.VMEM((count, rows, HD), F32),
            ],
        ),
    )


def rope_tables(positions):
    inverse = 1.0 / 10000.0 ** (jnp.arange(0, HD, 2).astype(F32) / HD)
    angle = positions.astype(F32)[:, None] * inverse[None, :]
    cos, sin = jnp.cos(angle), jnp.sin(angle)
    cos_head = jnp.concatenate([cos, cos], axis=1)
    sin_head = jnp.concatenate([-sin, sin], axis=1)
    ones, zeros = jnp.ones_like(cos_head), jnp.zeros_like(sin_head)
    return (
        jnp.concatenate([cos_head, cos_head], axis=1),
        jnp.concatenate([sin_head, sin_head], axis=1),
        jnp.concatenate([cos_head, ones], axis=1),
        jnp.concatenate([sin_head, zeros], axis=1),
    )


def normalize(values, gain):
    scale = lax.rsqrt(jnp.mean(values * values, axis=-1, keepdims=True) + EPSILON)
    return scale, (values * scale * gain).astype(BF)


def normalize_back(values, scale, gain, grad):
    norm = values * scale
    scaled = grad * gain
    inner = scale * (scaled - norm * jnp.mean(scaled * norm, axis=-1, keepdims=True))
    return inner, jnp.sum(grad * norm, axis=0)


class Sizes:
    def __init__(self, tokens, w_query):
        self.micro, self.held, self.width = tokens.shape
        self.rows = self.held // 2
        self.count = lax.axis_size("wide")
        self.depth = self.width // self.count
        self.heads = w_query.shape[2] // 2
        self.qkv = self.heads + PAIR


def shards(
    tokens, out_grad, attn_gain, w_query, w_key, w_value, w_out, ffn_gain, w_gate, w_up, w_down
):
    s = Sizes(tokens, w_query)
    section = lax.axis_index("section")
    wide = lax.axis_index("wide")
    core = lax.axis_index("tp")
    count, rows = s.count, s.rows
    home = section == 0

    pos = jnp.stack(
        [
            jnp.where((core ^ (p // 2)) == 0, 2 * wide, 2 * count - 1 - 2 * wide) * s.held
            + (section ^ (p % 2)) * rows
            for p in range(4)
        ]
    ).astype(jnp.int32)
    order = jnp.arange(4 * count)
    half_block = order // 2
    odd = half_block % 2
    owner = jnp.where(odd == 0, half_block, 2 * count - 1 - half_block) // 2
    loc = ((owner ^ wide) * 4 + (odd ^ core) * 2 + ((order % 2) ^ section)).astype(jnp.int32)
    positions = (pos[:, None] + jnp.arange(rows)[None, :]).reshape(-1)
    tables = rope_tables(positions)
    place = (tables, loc, pos)

    def halves(array, axis):
        size = array.shape[axis] // 2
        own = lax.dynamic_slice_in_dim(array, section * size, size, axis)
        away = lax.dynamic_slice_in_dim(array, (1 - section) * size, size, axis)
        return own, away

    def pack_attn(parts):
        query, key, value, out = parts
        main = jnp.concatenate([query, key, value, out.T], axis=1)
        gains = jnp.concatenate([attn_gain, ffn_gain], axis=0)
        gains = jnp.pad(gains, ((0, GAIN_ROWS - 2), (0, main.shape[1] - gains.shape[1])))
        return jnp.concatenate([main, gains], axis=0)

    def both_layers(own, away):
        other = partner(away, "section", 1)
        return jnp.where(home, own, other), jnp.where(home, other, own)

    def take(values):
        part = lax.dynamic_slice_in_dim(values, section * rows, rows, 1)
        return mirror(part).reshape(-1, s.width)

    attn = [halves(w_query[0], 1), halves(w_key[0], 1), halves(w_value[0], 1), halves(w_out[0], 0)]
    gate_h, up_h, down_h = halves(w_gate[0], 1), halves(w_up[0], 1), halves(w_down[0], 0)
    attn_l = both_layers(*[pack_attn([part[i] for part in attn]) for i in range(2)])
    gate_l = both_layers(*gate_h)
    up_l = both_layers(*up_h)
    down_l = both_layers(*[half.T for half in down_h])

    u = take(tokens).astype(F32)
    layers, kept, outs = [], [], []
    for layer in range(2):
        attn = lax.all_gather(
            after(attn_l[layer], *layers[0][2]) if layer else attn_l[layer],
            "wide",
            axis=0,
            tiled=True,
        )
        by_block = attn.reshape(count, s.depth + GAIN_ROWS, -1)
        gains = by_block[:, s.depth : s.depth + 2, : s.depth]
        gains = gains.transpose(1, 0, 2).reshape(2, s.width).astype(F32)
        first_scale, low = normalize(u, gains[0])
        normed = spread(low)
        line_gate = gather_line(after(gate_l[layer], attn))
        q, kv_own = qkv_project(normed, attn, tables, s.micro, s.depth, s.qkv)
        kv = jnp.concatenate(gather_blocks(kv_own), axis=0)
        line_up = gather_line(after(up_l[layer], kv))
        gate_w = (line_gate, partner(after(line_gate, kv), "wide", 1))
        attended, lse = attend(q, kv, loc, pos)
        flat = attended.reshape(-1, s.heads)
        own, send = contract([flat], [(attn,)], (s.qkv,), s.depth, s.width)
        line_down = gather_line(after(down_l[layer], line_up))
        up_w = (line_up, partner(after(line_up, gate_w[1], own), "wide", 1))
        middle = u + fold(own, send)
        second_scale, low = normalize(middle, gains[1])
        normed_ffn = spread(low)
        gate, up, hidden = gate_up(normed_ffn, gate_w, up_w, s.depth)
        down_w = (line_down, partner(after(line_down, up_w[1]), "wide", 1))
        own, send = contract([hidden], [down_w], (None,), s.depth, s.width)
        result = middle + fold(own, send)
        layers.append((gains, attn, gate_w, up_w, down_w))
        kept.append(
            (u, first_scale, normed, q, kv, attended, lse, middle, second_scale, normed_ffn)
            + (gate, up, hidden)
        )
        outs.append(result.astype(BF))
        u = outs[layer].astype(F32)

    def reduce(send, keep, *events):
        got = partner(after(send, *events), "wide", 1)
        near = (keep.astype(F32) + got.astype(F32)).astype(BF)
        return reduce_line(near.reshape(-1, near.shape[-1])).astype(F32)

    upstream = take(out_grad).astype(F32)
    grads, terms = [None, None], [None, None]
    for layer in (1, 0):
        gains, attn, gate_w, up_w, down_w = layers[layer]
        u, first_scale, normed, q, kv, attended, lse, middle, second_scale, normed_ffn = kept[
            layer
        ][:10]
        gate, up, hidden = kept[layer][10:]
        grad2 = spread(upstream.astype(BF))
        grad_gate, grad_up = hidden_back(grad2, down_w, gate, up, s.depth)
        own, send = contract(
            [grad_gate, grad_up], [gate_w, up_w], (None, None), s.depth, s.width
        )
        d_down = reduce(*weight_grad(grad2, hidden, count))
        inner, second_gain = normalize_back(middle, second_scale, gains[1], fold(own, send))
        grad_middle = upstream + inner
        grad1 = spread(grad_middle.astype(BF))
        d_gate = reduce(*weight_grad(normed_ffn, grad_gate, count))
        grad_attended = out_back(grad1, attn, s.depth, s.qkv, s.heads).reshape(q.shape)
        dq, send, keep = attend_back(
            q, grad_attended, attended, lse, kv, tables[0], tables[1], loc, pos
        )
        halved = lambda x: x.reshape(count // 2, 4, s.micro, rows, PAIR)
        dkv = reduce_blocks(halved(send), halved(keep))
        d_up = reduce(*weight_grad(normed_ffn, grad_up, count), dkv)
        half = HD // 2
        turned = jnp.concatenate(
            [dkv[..., half:HD], dkv[..., :half], jnp.zeros_like(dkv[..., HD:])], axis=-1
        )
        by_piece = lambda table: table.reshape(4, 1, rows, PAIR)
        dkv = (dkv * by_piece(tables[2]) - turned * by_piece(tables[3])).astype(BF)
        dq, dkv = dq.reshape(-1, s.heads), dkv.reshape(-1, PAIR)
        own, send = contract([dq, dkv], [(attn,), (attn,)], (0, s.heads), s.depth, s.width)
        inner, first_gain = normalize_back(u, first_scale, gains[0], fold(own, send))
        grads[layer] = (grad_middle + inner).astype(BF)
        gain_rows = jnp.stack([first_gain, second_gain]).astype(BF)
        gain_rows = gain_rows.reshape(2, count // 2, 2, s.depth).transpose(1, 2, 0, 3)
        gain_rows = jnp.pad(
            gain_rows,
            ((0, 0), (0, 0), (0, GAIN_ROWS - 2), (0, s.qkv + s.heads - s.depth)),
        )
        d_attn = reduce(
            *attn_weight_grad(
                normed, grad1, dq, dkv, attended.reshape(-1, s.heads), gain_rows, count
            )
        )
        terms[layer] = (d_attn, d_gate, d_up, d_down)
        upstream = grads[layer].astype(F32)

    def give(first, second):
        first, second = [x.reshape(s.micro, rows, s.width) for x in (first, second)]
        own = jnp.where(home, first, second)
        other = partner(jnp.where(home, second, first), "section", 1)
        both = jnp.concatenate(
            [jnp.where(home, own, other), jnp.where(home, other, own)], axis=1
        )
        return mirror(both)

    section_out = give(*outs)
    input_grads = give(*grads)

    def settle(index):
        first, second = terms[0][index], terms[1][index]
        own = jnp.where(home, first, second)
        other = partner(jnp.where(home, second, first).astype(BF), "section", 1).astype(F32)
        return jnp.where(home, own, other), jnp.where(home, other, own)

    depth, heads = s.depth, s.heads
    low, high = settle(0)
    cut = lambda start, size: jnp.concatenate(
        [low[:depth, start : start + size], high[:depth, start : start + size]], axis=1
    )
    d_query = cut(0, heads)
    d_key = cut(heads, HD)
    d_value = cut(heads + HD, HD)
    d_out = jnp.concatenate([low[:depth, s.qkv :].T, high[:depth, s.qkv :].T], axis=0)
    gains = (low + high)[depth : depth + 2, :depth]
    gains = gains + partner(gains, "tp", 1)
    d_gate = jnp.concatenate(settle(1), axis=1)
    d_up = jnp.concatenate(settle(2), axis=1)
    d_down = jnp.concatenate([half.T for half in settle(3)], axis=0)
    return (
        section_out[None],
        input_grads[None],
        gains[0:1],
        d_query[None],
        d_key[None],
        d_value[None],
        d_out[None],
        gains[1:2],
        d_gate[None],
        d_up[None],
        d_down[None],
    )


def solution(mesh):
    return jax.shard_map(
        shards,
        mesh=mesh,
        in_specs=(
            P(None, ("wide", "tp"), None),
            P(None, ("wide", "tp"), None),
            P("section", "wide"),
            P("section", "wide", "tp"),
            P("section", "wide", "tp"),
            P("section", "wide", "tp"),
            P("section", "tp", "wide"),
            P("section", "wide"),
            P("section", "wide", "tp"),
            P("section", "wide", "tp"),
            P("section", "tp", "wide"),
        ),
        out_specs=(
            P("section", None, ("wide", "tp"), None),
            P("section", None, ("wide", "tp"), None),
            P("section", "wide"),
            P("section", "wide", "tp"),
            P("section", "wide", "tp"),
            P("section", "wide", "tp"),
            P("section", "tp", "wide"),
            P("section", "wide"),
            P("section", "wide", "tp"),
            P("section", "wide", "tp"),
            P("section", "tp", "wide"),
        ),
        check_vma=False,
    )
```

```python
import functools
import math

import jax
import jax.numpy as jnp
from jax import lax
from jax.experimental import pallas as pl
from jax.experimental.pallas import tpu as pltpu
from jax.sharding import PartitionSpec as P

HD = 64
PAIR = 2 * HD
EPSILON = 1e-05
GAIN_ROWS = 16
VMEM = 48 * 2**20
BF = jnp.bfloat16
F32 = jnp.float32
ANY = pl.BlockSpec(memory_space=pl.ANY)


def partner(x, axis, bit):
    peers = lax.axis_size(axis)
    return lax.ppermute(x, axis, [(i, i ^ bit) for i in range(peers)])


def partner_one(x, source):
    return lax.ppermute(x, "section", [(source, 1 - source)])


def after(value, *events):
    return lax.optimization_barrier((value,) + events)[0]


def product(left, right):
    return jnp.dot(left, right, preferred_element_type=F32)


def cross(left, right):
    return lax.dot_general(left, right, (((0,), (0,)), ((), ())), preferred_element_type=F32)


def against(left, right):
    return lax.dot_general(left, right, (((1,), (1,)), ((), ())), preferred_element_type=F32)


def call(body, ins, outs, scratch, flops, exps=0, ident=None, light=False, **more):
    moved = sum(x.size * x.dtype.itemsize for x in list(ins) + list(outs))
    if light:
        moved, flops, exps = moved // 8, flops // 8, exps // 8
    remote = {} if ident is None else {"collective_id": ident, "has_side_effects": True}
    return pl.pallas_call(
        body,
        out_shape=outs,
        scratch_shapes=scratch,
        compiler_params=pltpu.CompilerParams(vmem_limit_bytes=VMEM, **remote),
        cost_estimate=pl.CostEstimate(
            flops=int(flops), bytes_accessed=int(moved), transcendentals=int(exps)
        ),
        **more,
    )(*ins)


def shaped(*dims, kind=BF):
    return jax.ShapeDtypeStruct(dims, kind)


def lines():
    count = lax.axis_size("wide")
    return [list(range(y, count, 2)) for y in range(2)]


def side():
    return lax.axis_index("wide") % 2


def gather_line(shard):
    return lax.all_gather(shard, "wide", axis=0, tiled=True, axis_index_groups=lines())


def reduce_line(near):
    return lax.psum_scatter(
        near, "wide", scatter_dimension=0, tiled=True, axis_index_groups=lines()
    )


def gather_blocks(shard):
    count = lax.axis_size("wide")
    far = [shard if k == 0 else partner(shard, "wide", k) for k in range(0, count, 2)]
    blocks = []
    for block in far:
        blocks += [block, partner(block, "wide", 1)]
    return blocks


def reduce_near(keep, got):
    return keep.astype(F32) + got.astype(F32)


def reduce_far(near):
    total = near[0]
    for j in range(1, near.shape[0]):
        total = total + partner(near[j].astype(BF), "wide", 2 * j).astype(F32)
    return total


def mirror(x, cross=0, sections=(0, 1)):
    count = lax.axis_size("wide")
    pairs = []
    for section in sections:
        for w in range(count):
            for core in range(2):
                to = w if core == 0 else count - 1 - w
                pairs.append(
                    ((section * count + w) * 2 + core, ((section ^ cross) * count + to) * 2 + core)
                )
    return lax.ppermute(x, ("section", "wide", "tp"), pairs)


def spread(values):
    other = partner(values, "section", 1)
    return [values, other, partner(values, "tp", 1), partner(other, "tp", 1)]


def fold(own, send):
    rows = own.shape[0] // 2
    got = partner(send, "tp", 1)
    away = (own[rows:].astype(F32) + got[rows:].astype(F32)).astype(BF)
    mine = own[:rows].astype(F32) + got[:rows].astype(F32)
    return mine + partner(away, "section", 1).astype(F32)


def load_attn(ref, dest, sem, start):
    copy = pltpu.make_async_copy(ref.at[:, pl.ds(start, dest.shape[1])], dest, sem.at[0])
    copy.start()
    return [copy]


def load_sides(refs, dest, sem, depth, first=0):
    copies = []
    if len(refs) == 1:
        copies.append(pltpu.make_async_copy(refs[0], dest, sem.at[first]))
        copies[-1].start()
        return copies
    y = side()
    for s, ref in enumerate(refs):
        for j in range(dest.shape[0] // (2 * depth)):
            place = pl.multiple_of((2 * j + (y + s) % 2) * depth, depth)
            copies.append(
                pltpu.make_async_copy(
                    ref.at[pl.ds(j * depth, depth)],
                    dest.at[pl.ds(place, depth)],
                    sem.at[first + 2 * j + s],
                )
            )
            copies[-1].start()
    return copies


def exchange_kernel(back, keep_f32, last, bulk, *refs):
    own_ref, send_ref, base_ref, gain_ref = refs[:4]
    refs = refs[4:]
    if back:
        values_ref, scale_ref = refs[:2]
        refs = refs[2:]
    bulk_in, refs = refs[:bulk], refs[bulk:]
    held = 1 if last else 4
    pieces, refs = refs[:held], refs[held:]
    first_out, second_out = refs[:2]
    bulk_out, refs = refs[2 : 2 + bulk], refs[2 + bulk :]
    got_tp, away, got_section, low, send_sem, recv_sem, local_sem, bulk_sem = refs
    rows, width = low.shape
    chunks = 4
    size = rows // chunks
    peers = {
        "tp": {"tp": 1 - lax.axis_index("tp")},
        "section": {"section": 1 - lax.axis_index("section")},
        "near": {"wide": lax.axis_index("wide") + 1 - 2 * side()},
    }
    greeted = ["tp", "section"] + (["near"] if bulk else [])
    barrier = pltpu.get_barrier_semaphore()
    for name in greeted:
        pl.semaphore_signal(
            barrier, inc=1, device_id=peers[name], device_id_type=pl.DeviceIdType.MESH
        )
    pl.semaphore_wait(barrier, len(greeted))

    def remote(source, target, index, name):
        copy = pltpu.make_async_remote_copy(
            src_ref=source,
            dst_ref=target,
            send_sem=send_sem.at[index],
            recv_sem=recv_sem.at[index],
            device_id=peers[name],
            device_id_type=pl.DeviceIdType.MESH,
        )
        copy.start()
        return copy

    bulk_copies = [
        pltpu.make_async_remote_copy(
            src_ref=bulk_in[i],
            dst_ref=bulk_out[i],
            send_sem=bulk_sem.at[0, i],
            recv_sem=bulk_sem.at[1, i],
            device_id=peers["near"],
            device_id_type=pl.DeviceIdType.MESH,
        )
        for i in range(bulk)
    ]
    for copy in bulk_copies:
        copy.start()
    span = lambda c: pl.ds(c * size, size)
    sums = [
        remote(send_ref.at[pl.ds(rows, rows)], got_tp.at[1], 0, "tp"),
        remote(send_ref.at[pl.ds(0, rows)], got_tp.at[0], 1, "tp"),
    ]
    sums[0].wait()
    crossing = []
    for c in range(chunks):
        total = own_ref[rows + c * size : rows + (c + 1) * size].astype(F32)
        away[span(c)] = (total + got_tp[1, span(c)].astype(F32)).astype(BF)
        crossing.append(remote(away.at[span(c)], got_section.at[span(c)], 2 + c, "section"))
    sums[1].wait()
    over_section, over_tp, local = [], [], []
    gain = gain_ref[...]
    gain_total = jnp.zeros((1, width), F32)
    for c in range(chunks):
        here = slice(c * size, (c + 1) * size)
        crossing[c].wait()
        total = own_ref[here].astype(F32) + got_tp[0, here].astype(F32)
        total = total + got_section[here].astype(F32)
        base = base_ref[here].astype(F32)
        if back:
            scale = scale_ref[here]
            norm = values_ref[here].astype(F32) * scale
            scaled = total * gain
            mean = jnp.mean(scaled * norm, axis=-1, keepdims=True)
            gain_total = gain_total + jnp.sum(total * norm, axis=0, keepdims=True)
            result = base + scale * (scaled - norm * mean)
            if keep_f32:
                first_out[here] = result
            low[here] = result.astype(BF)
        else:
            result = base + total
            if keep_f32:
                first_out[here] = result
            else:
                first_out[here] = result.astype(BF)
                result = result.astype(BF).astype(F32)
            scale = lax.rsqrt(jnp.mean(result * result, axis=-1, keepdims=True) + EPSILON)
            second_out[here] = scale
            low[here] = (result * scale * gain).astype(BF)
        copy = pltpu.make_async_copy(low.at[span(c)], pieces[0].at[span(c)], local_sem.at[c])
        copy.start()
        local.append(copy)
        if last:
            continue
        over_section.append(
            remote(low.at[span(c)], pieces[1].at[span(c)], 2 + chunks + c, "section")
        )
        over_tp.append(remote(low.at[span(c)], pieces[2].at[span(c)], 2 + 2 * chunks + c, "tp"))
    if back:
        second_out[...] = gain_total
        if not keep_f32:
            first_out[...] = gain_total
    forwarded = []
    for c in range(0 if last else chunks):
        over_section[c].wait()
        forwarded.append(
            remote(pieces[1].at[span(c)], pieces[3].at[span(c)], 2 + 3 * chunks + c, "tp")
        )
    for copy in local + over_tp + forwarded + bulk_copies:
        copy.wait()


def exchange(
    own, send, base, gain, values=None, scale=None, keep_f32=True, last=False, bulk=(), ident=0
):
    rows, width = base.shape
    back = values is not None
    vmem = pl.BlockSpec(memory_space=pltpu.VMEM)
    ins = [own, send, base, gain.reshape(1, width)] + ([values, scale] if back else [])
    piece = shaped(rows, width)
    if back:
        first = shaped(rows, width, kind=F32) if keep_f32 else shaped(1, width, kind=F32)
        second = shaped(1, width, kind=F32)
    else:
        first = shaped(rows, width, kind=F32 if keep_f32 else BF)
        second = shaped(rows, 1, kind=F32)
    count = 2 + 4 * 4
    held = 1 if last else 4
    outs = call(
        functools.partial(exchange_kernel, back, keep_f32, last, len(bulk)),
        [*ins, *bulk],
        [piece] * held + [first, second] + [shaped(*x.shape) for x in bulk],
        [
            pltpu.VMEM((2, rows, width), BF),
            pltpu.VMEM((rows, width), BF),
            pltpu.VMEM((rows, width), BF),
            pltpu.VMEM((rows, width), BF),
            pltpu.SemaphoreType.DMA((count,)),
            pltpu.SemaphoreType.DMA((count,)),
            pltpu.SemaphoreType.DMA((4,)),
            pltpu.SemaphoreType.DMA((2, max(1, len(bulk)))),
        ],
        60e9,
        ident=ident,
        light=back,
        in_specs=[vmem] * len(ins) + [ANY] * len(bulk),
        out_specs=[ANY] * held + [vmem] * 2 + [ANY] * len(bulk),
    )
    return outs[:held], outs[held], outs[held + 1], outs[held + 2 :]


def qkv_kernel(*refs):
    pieces, attn, tables = refs[:4], refs[4], refs[5:9]
    q_ref, kv_ref, w, sem = refs[9:]
    width = w.shape[1]
    for copy in load_attn(attn, w, sem, 0):
        copy.wait()
    cos, sin, cos_kv, sin_kv = tables
    for p, piece in enumerate(pieces):
        linear = product(piece[...], w[...])
        micro, rows = q_ref.shape[1], q_ref.shape[2]
        first = lax.broadcasted_iota(jnp.int32, (rows, PAIR), 1) % HD < HD // 2
        span = slice(p * rows, (p + 1) * rows)
        for m in range(micro):
            for start in range(0, width, PAIR):
                part = linear[m * rows : (m + 1) * rows, start : start + PAIR]
                turned = jnp.where(
                    first, pltpu.roll(part, PAIR - HD // 2, 1), pltpu.roll(part, HD // 2, 1)
                )
                if start + PAIR < width:
                    out = part * cos[span] + turned * sin[span]
                    q_ref[p, m, :, start : start + PAIR] = out.astype(BF)
                else:
                    out = part * cos_kv[span] + turned * sin_kv[span]
                    kv_ref[p, m] = out.astype(BF)


def qkv_project(pieces, attn, tables, micro, width):
    total, d = pieces[0].shape
    rows = total // micro
    vmem = pl.BlockSpec(memory_space=pltpu.VMEM)
    return call(
        qkv_kernel,
        [*pieces, attn, *tables],
        [shaped(4, micro, rows, width - PAIR), shaped(4, micro, rows, PAIR)],
        [pltpu.VMEM((d, width), BF), pltpu.SemaphoreType.DMA((1,))],
        8 * total * d * width,
        in_specs=[vmem] * 4 + [ANY] + [vmem] * 4,
        out_specs=[vmem] * 2,
    )


def gate_up_kernel(depth, sides, *refs):
    pieces, refs = refs[:4], refs[4:]
    gates, ups, refs = refs[: sides[0]], refs[sides[0] : sum(sides)], refs[sum(sides) :]
    outs = refs[:3]
    x, w_gate, w_up, buffer, x_sem, w_sem, out_sem = refs[3:]
    copies = load_sides(gates, w_gate, w_sem, depth)
    copies += load_sides(ups, w_up, w_sem, depth, w_gate.shape[0] // depth)
    inputs = []
    for p, piece in enumerate(pieces):
        inputs.append(pltpu.make_async_copy(piece, x.at[p], x_sem.at[p]))
        inputs[-1].start()
    for copy in copies:
        copy.wait()
    rows = x.shape[1]
    results = []
    for p in range(4):
        inputs[p].wait()
        gate = product(x[p], w_gate[...])
        up = product(x[p], w_up[...])
        if p >= 2:
            for copy in results[p - 2]:
                copy.wait()
        slot = p % 2
        buffer[slot, 0] = gate.astype(BF)
        buffer[slot, 1] = up.astype(BF)
        buffer[slot, 2] = (gate * jax.nn.sigmoid(gate) * up).astype(BF)
        results.append(
            [
                pltpu.make_async_copy(
                    buffer.at[slot, i], outs[i].at[pl.ds(p * rows, rows)], out_sem.at[p, i]
                )
                for i in range(3)
            ]
        )
        for copy in results[p]:
            copy.start()
    for p in (2, 3):
        for copy in results[p]:
            copy.wait()


def gate_up(pieces, gates, ups, depth):
    rows, d = pieces[0].shape
    hidden = gates[0].shape[1]
    return call(
        functools.partial(gate_up_kernel, depth, (len(gates), len(ups))),
        [*pieces, *gates, *ups],
        [shaped(4 * rows, hidden)] * 3,
        [
            pltpu.VMEM((4, rows, d), BF),
            pltpu.VMEM((d, hidden), BF),
            pltpu.VMEM((d, hidden), BF),
            pltpu.VMEM((2, 3, rows, hidden), BF),
            pltpu.SemaphoreType.DMA((4,)),
            pltpu.SemaphoreType.DMA((2 * d // depth,)),
            pltpu.SemaphoreType.DMA((4, 3)),
        ],
        16 * rows * d * hidden,
        4 * rows * hidden,
        in_specs=[ANY] * (4 + len(gates) + len(ups)),
        out_specs=[ANY] * 3,
    )


def hidden_back_kernel(depth, *refs):
    pieces, downs = refs[:4], refs[4:6]
    gate_ref, up_ref = refs[6:8]
    outs = refs[8:10]
    x, w, kept, buffer, x_sem, w_sem, kept_sem, out_sem = refs[10:]
    copies = load_sides(downs, w, w_sem, depth)
    rows = x.shape[1]
    inputs = []
    for p, piece in enumerate(pieces):
        span = pl.ds(p * rows, rows)
        inputs.append(
            [
                pltpu.make_async_copy(piece, x.at[p], x_sem.at[p]),
                pltpu.make_async_copy(gate_ref.at[span], kept.at[p, 0], kept_sem.at[p, 0]),
                pltpu.make_async_copy(up_ref.at[span], kept.at[p, 1], kept_sem.at[p, 1]),
            ]
        )
        for copy in inputs[-1]:
            copy.start()
    for copy in copies:
        copy.wait()
    results = []
    for p in range(4):
        for copy in inputs[p]:
            copy.wait()
        grad = product(x[p], w[...])
        gate = kept[p, 0].astype(F32)
        up = kept[p, 1].astype(F32)
        sigma = jax.nn.sigmoid(gate)
        if p >= 2:
            for copy in results[p - 2]:
                copy.wait()
        slot = p % 2
        buffer[slot, 0] = (grad * up * sigma * (1.0 + gate * (1.0 - sigma))).astype(BF)
        buffer[slot, 1] = (grad * gate * sigma).astype(BF)
        results.append(
            [
                pltpu.make_async_copy(
                    buffer.at[slot, i], outs[i].at[pl.ds(p * rows, rows)], out_sem.at[p, i]
                )
                for i in range(2)
            ]
        )
        for copy in results[p]:
            copy.start()
    for p in (2, 3):
        for copy in results[p]:
            copy.wait()


def hidden_back(pieces, downs, gate, up, depth):
    rows, d = pieces[0].shape
    hidden = downs[0].shape[1]
    return call(
        functools.partial(hidden_back_kernel, depth),
        [*pieces, *downs, gate, up],
        [shaped(4 * rows, hidden)] * 2,
        [
            pltpu.VMEM((4, rows, d), BF),
            pltpu.VMEM((d, hidden), BF),
            pltpu.VMEM((4, 2, rows, hidden), BF),
            pltpu.VMEM((2, 2, rows, hidden), BF),
            pltpu.SemaphoreType.DMA((4,)),
            pltpu.SemaphoreType.DMA((d // depth,)),
            pltpu.SemaphoreType.DMA((4, 2)),
            pltpu.SemaphoreType.DMA((4, 2)),
        ],
        8 * rows * d * hidden,
        4 * rows * hidden,
        in_specs=[ANY] * 8,
        out_specs=[ANY] * 2,
        light=True,
    )


def out_back_kernel(offset, *refs):
    pieces, attn = refs[:4], refs[4]
    out_ref, w, sem = refs[5:]
    for copy in load_attn(attn, w, sem, offset):
        copy.wait()
    rows = pieces[0].shape[0]
    for p, piece in enumerate(pieces):
        out_ref[p * rows : (p + 1) * rows] = product(piece[...], w[...]).astype(BF)


def out_back(pieces, attn, offset, width):
    rows, d = pieces[0].shape
    vmem = pl.BlockSpec(memory_space=pltpu.VMEM)
    return call(
        functools.partial(out_back_kernel, offset),
        [*pieces, attn],
        [shaped(4 * rows, width)],
        [pltpu.VMEM((d, width), BF), pltpu.SemaphoreType.DMA((1,))],
        8 * rows * d * width,
        in_specs=[vmem] * 4 + [ANY],
        out_specs=[vmem],
        light=True,
    )[0]


def contract_kernel(depth, starts, sizes, *refs):
    sides = len(starts)
    lefts, refs = refs[:sides], refs[sides:]
    sources = []
    for size in sizes:
        sources.append(refs[:size])
        refs = refs[size:]
    own_ref, send_ref = refs[:2]
    weights, sem = refs[2:-1], refs[-1]
    step = pl.program_id(0)
    half = pl.num_programs(0) // 2

    @pl.when(step == 0)
    def _():
        copies = []
        for s, start in enumerate(starts):
            if start is None:
                copies += load_sides(sources[s], weights[s], sem.at[s], depth)
            else:
                copies += load_attn(sources[s][0], weights[s], sem.at[s], start)
        for copy in copies:
            copy.wait()

    total = against(lefts[0][...], weights[0][...])
    for s in range(1, sides):
        total = total + against(lefts[s][...], weights[s][...])
    total = total.astype(BF)

    @pl.when(step < half)
    def _():
        send_ref[...] = total

    @pl.when(step >= half)
    def _():
        own_ref[...] = total


def contract(lefts, sources, starts, depth, width):
    sides = len(lefts)
    total = lefts[0].shape[0]
    tile = total // 4
    flat = [ref for group in sources for ref in group]
    return call(
        functools.partial(contract_kernel, depth, starts, [len(group) for group in sources]),
        [*lefts, *flat],
        [shaped(total // 2, width)] * 2,
        [pltpu.VMEM((width, left.shape[1]), BF) for left in lefts]
        + [pltpu.SemaphoreType.DMA((sides, width // depth))],
        sum(2 * total * left.shape[1] * width for left in lefts),
        grid=(4,),
        in_specs=[
            pl.BlockSpec((tile, left.shape[1]), lambda i: ((i + 2) % 4, 0)) for left in lefts
        ]
        + [ANY] * len(flat),
        out_specs=[
            pl.BlockSpec((tile, width), lambda i: (jnp.maximum(i - 2, 0), 0)),
            pl.BlockSpec((tile, width), lambda i: (jnp.minimum(i, 1), 0)),
        ],
    )


def weight_kernel(rights, split, *refs):
    pieces, right_refs, outs = refs[:4], refs[4 : 4 + rights], refs[4 + rights :]
    left = jnp.concatenate([x[...] for x in pieces], axis=0)
    start = 0
    for right in right_refs:
        grad = cross(left, right[...]).astype(BF)
        span = slice(start, start + right.shape[1])
        start += right.shape[1]
        if not split:
            outs[0][:, span] = grad
            continue
        send_ref, keep_ref = outs
        depth = keep_ref.shape[1]
        for y, (first, second) in enumerate(((keep_ref, send_ref), (send_ref, keep_ref))):

            @pl.when(side() == y)
            def _():
                first[0, :, span] = grad[:depth]
                second[0, :, span] = grad[depth:]


def weight_grad(pieces, rights, n, split=True):
    rows, d = pieces[0].shape
    width = sum(right.shape[1] for right in rights)
    depth = d // n
    if split:
        shapes = [shaped(n // 2, depth, width)] * 2
        specs = [pl.BlockSpec((1, depth, width), lambda j: (j, 0, 0))] * 2
    else:
        shapes = [shaped(d, width)]
        specs = [pl.BlockSpec((2 * depth, width), lambda j: (j, 0))]
    outs = call(
        functools.partial(weight_kernel, len(rights), split),
        [*pieces, *rights],
        shapes,
        [],
        8 * rows * d * width,
        grid=(n // 2,),
        in_specs=[pl.BlockSpec((rows, 2 * depth), lambda j: (0, j))] * 4
        + [pl.BlockSpec(right.shape, lambda j: (0, 0)) for right in rights],
        out_specs=specs,
        light=True,
    )
    return outs if split else outs[0]


def stack_heads(x):
    return jnp.concatenate([x[:, h : h + HD] for h in range(0, x.shape[1], HD)], axis=0)


def turn_heads(x):
    pairs = [x[:, g : g + PAIR].T for g in range(0, x.shape[1], PAIR)]
    return jnp.concatenate([part for pair in pairs for part in (pair[:HD], pair[HD:])], axis=1)


def back_heads(x, rows, g):
    even = x[:, 2 * g * rows : (2 * g + 1) * rows]
    odd = x[:, (2 * g + 1) * rows : (2 * g + 2) * rows]
    return jnp.concatenate([even, odd], axis=0).T


def attend_kernel(
    block, loc_ref, pos_ref, q_ref, kv_ref, o_ref, lse_ref, k_ref, vt_ref, m_ref, acc_ref
):
    piece = pl.program_id(1)
    rows = q_ref.shape[2]
    count = kv_ref.shape[0]
    per_block = block // rows

    @pl.when(piece == 0)
    def _():
        def one(i, _):
            kv = kv_ref[loc_ref[i], 0]
            k_ref[i] = kv[:, :HD]
            ones = jnp.ones((GAIN_ROWS, rows), BF)
            vt_ref[i] = jnp.concatenate([kv.T[HD:], ones], axis=0)
            return 0

        lax.fori_loop(0, count, one, 0)

    pos = pos_ref[piece]
    queries = turn_heads(q_ref[0, 0] * BF(1.0 / math.sqrt(HD)))
    m_ref[...] = jnp.full(m_ref.shape, -1e30, F32)
    acc_ref[...] = jnp.zeros(acc_ref.shape, F32)

    def step(j, masked):
        first = j * per_block
        keys = jnp.concatenate([k_ref[first + i] for i in range(per_block)], axis=0)
        values = jnp.concatenate([vt_ref[first + i] for i in range(per_block)], axis=1)
        scores = product(keys, queries)
        if masked:
            row = lax.broadcasted_iota(jnp.int32, scores.shape, 0)
            column = lax.broadcasted_iota(jnp.int32, scores.shape, 1) % rows
            scores = jnp.where(row + j * block <= column + pos, scores, -1e30)
        before = m_ref[...]
        now = jnp.maximum(before, jnp.max(scores, axis=0, keepdims=True))
        terms = jnp.exp(scores - now)
        shrink = jnp.exp(before - now)
        acc_ref[...] = acc_ref[...] * shrink + product(values, terms.astype(BF))
        m_ref[...] = now

    full = pos // block

    def loop(j, _):
        step(j, False)
        return 0

    lax.fori_loop(0, full, loop, 0)
    step(full, True)
    total = acc_ref[HD : HD + 1]
    out = acc_ref[:HD] / total
    lse_ref[0, 0] = m_ref[...] + jnp.log(total)
    for g in range(q_ref.shape[3] // PAIR):
        o_ref[0, 0, :, g * PAIR : (g + 1) * PAIR] = back_heads(out, rows, g).astype(BF)


def attend(q, kv, loc, pos):
    pieces, micro, rows, width = q.shape
    count = kv.shape[0]
    stacked = rows * width // HD
    block = min(512, rows * count)
    scores = micro * pieces * stacked * rows * count // 2
    heads = pl.BlockSpec((1, 1, rows, width), lambda m, p, *_: (p, m, 0, 0))
    return call(
        functools.partial(attend_kernel, block),
        [loc, pos, q, kv],
        [shaped(*q.shape), shaped(pieces, micro, 1, stacked, kind=F32)],
        (),
        scores * 2750,
        scores,
        grid_spec=pltpu.PrefetchScalarGridSpec(
            num_scalar_prefetch=2,
            grid=(micro, pieces),
            in_specs=[
                heads,
                pl.BlockSpec((count, 1, rows, PAIR), lambda m, p, *_: (0, m, 0, 0)),
            ],
            out_specs=[
                heads,
                pl.BlockSpec((1, 1, 1, stacked), lambda m, p, *_: (p, m, 0, 0)),
            ],
            scratch_shapes=[
                pltpu.VMEM((count, rows, HD), BF),
                pltpu.VMEM((count, HD + GAIN_ROWS, rows), BF),
                pltpu.VMEM((1, stacked), F32),
                pltpu.VMEM((HD + GAIN_ROWS, stacked), F32),
            ],
        ),
    )


def attend_back_kernel(
    block,
    loc_ref,
    pos_ref,
    q_ref,
    do_ref,
    o_ref,
    lse_ref,
    kv_ref,
    cos_ref,
    sin_ref,
    before_ref,
    dq_ref,
    send_ref,
    keep_ref,
    k_ref,
    v_ref,
    kt_ref,
    dq_acc,
    dk_acc,
    dv_acc,
):
    piece = pl.program_id(0)
    rows = q_ref.shape[2]
    count = kv_ref.shape[0]
    per_block = block // rows
    scale = 1.0 / math.sqrt(HD)

    @pl.when(piece == 0)
    def _():
        def one(i, _):
            kv = kv_ref[loc_ref[i], 0]
            k_ref[i] = kv[:, :HD]
            v_ref[i] = kv[:, HD:]
            kt_ref[i] = kv.T[:HD]
            dk_acc[i] = jnp.zeros(dk_acc.shape[1:], F32)
            dv_acc[i] = jnp.zeros(dv_acc.shape[1:], F32)
            return 0

        lax.fori_loop(0, count, one, 0)

    pos = pos_ref[piece]
    q = q_ref[0, 0] * BF(scale)
    do = do_ref[0, 0]
    queries, queries_t = stack_heads(q), turn_heads(q)
    grads, grads_t = stack_heads(do), turn_heads(do)
    dots = turn_heads(do.astype(F32) * o_ref[0, 0].astype(F32))
    delta = jnp.sum(dots, axis=0, keepdims=True)
    logs = lse_ref[0, 0]
    dq_acc[...] = jnp.zeros(dq_acc.shape, F32)

    def step(j, masked):
        first = j * per_block
        keys = jnp.concatenate([k_ref[first + i] for i in range(per_block)], axis=0)
        values = jnp.concatenate([v_ref[first + i] for i in range(per_block)], axis=0)
        keys_t = jnp.concatenate([kt_ref[first + i] for i in range(per_block)], axis=1)
        scores = product(keys, queries_t)
        probs = jnp.exp(scores - logs)
        if masked:
            row = lax.broadcasted_iota(jnp.int32, scores.shape, 0)
            column = lax.broadcasted_iota(jnp.int32, scores.shape, 1) % rows
            probs = jnp.where(row + j * block <= column + pos, probs, 0.0)
        grad_probs = product(values, grads_t)
        grad_low = (probs * (grad_probs - delta)).astype(BF)
        dv = product(probs.astype(BF), grads)
        dk = product(grad_low, queries)
        dq_acc[...] += product(keys_t, grad_low)
        for i in range(per_block):
            dk_acc[first + i] += dk[i * rows : (i + 1) * rows]
            dv_acc[first + i] += dv[i * rows : (i + 1) * rows]

    full = pos // block

    def loop(j, _):
        step(j, False)
        return 0

    lax.fori_loop(0, full, loop, 0)
    step(full, True)

    first = lax.broadcasted_iota(jnp.int32, (rows, PAIR), 1) % HD < HD // 2
    for g in range(q_ref.shape[3] // PAIR):
        part = back_heads(dq_acc[...], rows, g) * scale
        turned = jnp.where(
            first, pltpu.roll(part, PAIR - HD // 2, 1), pltpu.roll(part, HD // 2, 1)
        )
        out = part * cos_ref[...] - turned * sin_ref[...]
        dq_ref[0, 0, :, g * PAIR : (g + 1) * PAIR] = out.astype(BF)

    @pl.when(piece == pl.num_programs(0) - 1)
    def _():
        pieces = pl.num_programs(0)

        def one(i, _):
            grad = jnp.concatenate([dk_acc[i], dv_acc[i]], axis=1).astype(BF)
            place = loc_ref[i]
            owner = place // pieces
            slot = owner // 2 * pieces + place % pieces

            @pl.when(owner % 2 == 0)
            def _():
                keep_ref[slot] = grad

            @pl.when(owner % 2 == 1)
            def _():
                send_ref[slot] = grad

            return 0

        lax.fori_loop(0, count, one, 0)


def attend_back(m, q, grad, attended, lse, kv, cos, sin, loc, pos, before):
    pieces, micro, rows, width = q.shape
    count = kv.shape[0]
    stacked = rows * width // HD
    block = min(512, rows * count)
    scores = pieces * stacked * rows * count // 2
    heads = pl.BlockSpec((1, 1, rows, width), lambda p, *_: (p, m, 0, 0))
    half = pl.BlockSpec((count // 2, rows, PAIR), lambda p, *_: (0, 0, 0))
    table = pl.BlockSpec((rows, PAIR), lambda p, *_: (p, 0))
    return call(
        functools.partial(attend_back_kernel, block),
        [loc, pos, q, grad, attended, lse, kv, cos, sin, before],
        [shaped(*q.shape)] + [shaped(count // 2, rows, PAIR)] * 2,
        (),
        scores * 4600,
        scores,
        input_output_aliases={9: 0} if m else {},
        grid_spec=pltpu.PrefetchScalarGridSpec(
            num_scalar_prefetch=2,
            grid=(pieces,),
            in_specs=[
                heads,
                heads,
                heads,
                pl.BlockSpec((1, 1, 1, stacked), lambda p, *_: (p, m, 0, 0)),
                pl.BlockSpec((count, 1, rows, PAIR), lambda p, *_: (0, m, 0, 0)),
                table,
                table,
                ANY,
            ],
            out_specs=[heads, half, half],
            scratch_shapes=[
                pltpu.VMEM((count, rows, HD), BF),
                pltpu.VMEM((count, rows, HD), BF),
                pltpu.VMEM((count, HD, rows), BF),
                pltpu.VMEM((HD, stacked), F32),
                pltpu.VMEM((count, rows, HD), F32),
                pltpu.VMEM((count, rows, HD), F32),
            ],
        ),
        light=True,
    )


def rope_tables(positions):
    inverse = 1.0 / 10000.0 ** (jnp.arange(0, HD, 2).astype(F32) / HD)
    angle = positions.astype(F32)[:, None] * inverse[None, :]
    cos, sin = jnp.cos(angle), jnp.sin(angle)
    cos_head = jnp.concatenate([cos, cos], axis=1)
    sin_head = jnp.concatenate([-sin, sin], axis=1)
    ones, zeros = jnp.ones_like(cos_head), jnp.zeros_like(sin_head)
    return (
        jnp.concatenate([cos_head, cos_head], axis=1),
        jnp.concatenate([sin_head, sin_head], axis=1),
        jnp.concatenate([cos_head, ones], axis=1),
        jnp.concatenate([sin_head, zeros], axis=1),
    )


def normalize(values, gain):
    scale = lax.rsqrt(jnp.mean(values * values, axis=-1, keepdims=True) + EPSILON)
    return scale, (values * scale * gain).astype(BF)


def normalize_back(values, scale, gain, grad):
    norm = values * scale
    scaled = grad * gain
    inner = scale * (scaled - norm * jnp.mean(scaled * norm, axis=-1, keepdims=True))
    return inner, jnp.sum(grad * norm, axis=0)


class Sizes:
    def __init__(self, tokens, w_query):
        self.micro, self.held, self.width = tokens.shape
        self.rows = self.held // 2
        self.count = lax.axis_size("wide")
        self.depth = self.width // self.count
        self.heads = w_query.shape[2] // 2
        self.qkv = self.heads + PAIR


def shards(
    tokens, out_grad, attn_gain, w_query, w_key, w_value, w_out, ffn_gain, w_gate, w_up, w_down
):
    s = Sizes(tokens, w_query)
    section = lax.axis_index("section")
    wide = lax.axis_index("wide")
    core = lax.axis_index("tp")
    count, rows = s.count, s.rows
    home = section == 0

    pos = jnp.stack(
        [
            jnp.where((core ^ (p // 2)) == 0, 2 * wide, 2 * count - 1 - 2 * wide) * s.held
            + (section ^ (p % 2)) * rows
            for p in range(4)
        ]
    ).astype(jnp.int32)
    order = jnp.arange(4 * count)
    half_block = order // 2
    odd = half_block % 2
    owner = jnp.where(odd == 0, half_block, 2 * count - 1 - half_block) // 2
    loc = ((owner ^ wide) * 4 + (odd ^ core) * 2 + ((order % 2) ^ section)).astype(jnp.int32)
    positions = (pos[:, None] + jnp.arange(rows)[None, :]).reshape(-1)
    tables = rope_tables(positions)
    place = (tables, loc, pos)

    def halves(array, axis):
        size = array.shape[axis] // 2
        own = lax.dynamic_slice_in_dim(array, section * size, size, axis)
        away = lax.dynamic_slice_in_dim(array, (1 - section) * size, size, axis)
        return own, away

    def pack_attn(parts):
        query, key, value, out = parts
        return jnp.concatenate([query, key, value, out.T], axis=1)

    def both_layers(own, away):
        other = partner(away, "section", 1)
        return jnp.where(home, own, other), jnp.where(home, other, own)

    def take(values):
        part = lax.dynamic_slice_in_dim(values, section * rows, rows, 1)
        return mirror(part).reshape(-1, s.width)

    own_gains = jnp.concatenate([attn_gain, ffn_gain], axis=0)
    own_gains = lax.all_gather(own_gains, "wide", axis=1, tiled=True)
    gains_l = [gains.astype(F32) for gains in both_layers(own_gains, own_gains)]
    attn = [halves(w_query[0], 1), halves(w_key[0], 1), halves(w_value[0], 1), halves(w_out[0], 0)]
    attn_l = both_layers(*[pack_attn([part[i] for part in attn]) for i in range(2)])
    gate_h = halves(w_gate[0], 1)
    gate_l = both_layers(gate_h[0], after(gate_h[1], attn_l[0]))
    u = take(tokens).astype(F32)
    first_scale, low = normalize(u, gains_l[0][0])
    normed = spread(low)
    up_h, down_h = halves(w_up[0], 1), halves(w_down[0], 0)
    up_l = both_layers(up_h[0], after(up_h[1], normed[1]))
    down_l = both_layers(down_h[0].T, after(down_h[1].T, up_l[0]))

    gather_all = lambda x: lax.all_gather(x, "wide", axis=0, tiled=True)
    near = lambda x, *events: partner(after(x, *events), "wide", 1)
    attn_0 = gather_all(attn_l[0])
    gate_0 = gather_line(gate_l[0])
    up_0 = gather_line(up_l[0])
    q0, kv_own = qkv_project(normed, attn_0, tables, s.micro, s.qkv)
    down_0 = gather_line(after(down_l[0], q0))
    kv0 = jnp.concatenate(gather_blocks(kv_own), axis=0)
    attn_1 = gather_all(after(attn_l[1], q0))
    attended0, lse0 = attend(q0, after(kv0, gate_0), loc, pos)
    gate_0 = (gate_0, near(gate_0, kv0))
    gate_1 = gather_line(after(gate_l[1], attended0))
    own, send = contract(
        [after(attended0, gate_0[1]).reshape(-1, s.heads)],
        [(attn_0,)],
        (s.qkv,),
        s.depth,
        s.width,
    )
    up_0 = (up_0, near(up_0, gate_0[1], own))
    upstream = take(after(out_grad, own))
    normed_ffn0, middle0, second_scale0, _ = exchange(
        after(own, down_0), send, u, gains_l[0][1], ident=0
    )
    up_1 = gather_line(after(up_l[1], middle0))
    down_0 = (down_0, near(down_0, up_0[1], middle0))
    gate0, up0, hidden0 = gate_up(
        [after(normed_ffn0[0], up_0[1], upstream), *normed_ffn0[1:]], (gate_0), up_0, s.depth
    )
    upstream_other = after(partner(after(upstream, up_0[1]), "section", 1), hidden0)
    down_1 = gather_line(after(down_l[1], hidden0))
    gate_1 = (gate_1, near(gate_1, down_0[1]))
    own, send = contract(
        [after(hidden0, upstream_other, attn_1)], [down_0], (None,), s.depth, s.width
    )
    kept0 = (u, first_scale, normed, q0, kv0, attended0, lse0, middle0, second_scale0)
    kept0 += (normed_ffn0, gate0, up0, hidden0)
    normed, u, first_scale, _ = exchange(
        after(own, gate_1[0]), send, middle0, gains_l[1][0], keep_f32=False, ident=1
    )
    out0 = u
    q1, kv_own = qkv_project(
        [after(normed[0], gate_1[1]), *normed[1:]], attn_1, tables, s.micro, s.qkv
    )
    kv1 = jnp.concatenate(gather_blocks(kv_own), axis=0)
    up_1 = (up_1, near(up_1, kv1))
    attended1, lse1 = attend(q1, after(kv1, up_1[0]), loc, pos)
    own, send = contract(
        [after(attended1, up_1[1], down_1).reshape(-1, s.heads)], [(attn_1,)], (s.qkv,), s.depth, s.width
    )
    down_1 = (down_1, near(down_1, up_1[1], own))
    normed_ffn1, middle1, second_scale1, _ = exchange(own, send, u, gains_l[1][1], ident=5)
    grad2 = [upstream, upstream_other]
    grad2 += [partner(after(x, normed_ffn1[0]), "tp", 1) for x in grad2]
    gate1, up1, hidden1 = gate_up(
        [after(normed_ffn1[0], down_1[1]), *normed_ffn1[1:]], gate_1, up_1, s.depth
    )
    kept1 = (u, first_scale, normed, q1, kv1, attended1, lse1, middle1, second_scale1)
    kept1 += (normed_ffn1, gate1, up1, hidden1)
    own1, send1 = contract([hidden1], [down_1], (None,), s.depth, s.width)
    layers = [
        (gains_l[0], attn_0, gate_0, up_0, down_0),
        (gains_l[1], attn_1, gate_1, up_1, down_1),
    ]
    kept = [kept0, kept1]

    def near_sum(keep, got):
        total = (keep.astype(F32) + got.astype(F32)).astype(BF)
        return total.reshape(-1, total.shape[-1])

    reduce_all = lambda x: lax.psum_scatter(x, "wide", scatter_dimension=0, tiled=True)

    def give(value, layer):
        value = value.reshape(s.micro, rows, s.width)
        pair = [mirror(value, 0, (layer,)), mirror(value, 1, (1 - layer,))]
        return jnp.concatenate(pair[::-1] if layer else pair, axis=1)

    grads, terms, gain_terms = [None, None], [None, None], []
    by_piece = lambda table: table.reshape(4, rows, PAIR)
    halved = lambda x: x.reshape(count // 2, 4, rows, PAIR)
    for layer in (1, 0):
        gains, attn, gate_w, up_w, down_w = layers[layer]
        u, first_scale, normed, q, kv, attended, lse, middle, second_scale, normed_ffn = kept[
            layer
        ][:10]
        gate, up, hidden = kept[layer][10:]
        flat = attended.reshape(-1, s.heads)
        if layer:
            grad2 = [after(x, own1) for x in grad2]
            given0 = give(after(out0, own1), 0)
        down_send, down_keep = weight_grad(grad2, [hidden], count)
        down_got = partner(down_send, "wide", 1)
        grad_gate, grad_up = hidden_back(
            [after(x, down_send) for x in grad2], down_w, gate, up, s.depth
        )
        gate_send, gate_keep = weight_grad(normed_ffn, [grad_gate], count)
        up_send, up_keep = weight_grad(
            [after(x, gate_send) for x in normed_ffn], [grad_up], count
        )
        if layer:
            out1 = (middle1 + fold(own1, send1)).astype(BF)
            grad_gate, given0 = lax.optimization_barrier((after(grad_gate, out1), given0))
        own, send = contract(
            [after(grad_gate, up_send), grad_up],
            [gate_w, up_w],
            (None, None),
            s.depth,
            s.width,
        )
        down_near = near_sum(down_keep, after(down_got, own))
        if layer == 0:
            own = after(own, d_attn)
            terms[1][0] = d_attn
        d_down = reduce_line(down_near)
        gate_got = partner(after(gate_send, down_near), "wide", 1)
        grad1, grad_middle, second_gain, _ = exchange(
            after(own, down_near), send, upstream, gains[1], middle, second_scale, ident=2
        )
        gate_got, d_down = after((gate_got, d_down), grad1[0])
        gate_near = near_sum(gate_keep, gate_got)
        d_gate = reduce_line(gate_near)
        up_got = partner(after(up_send, gate_near, d_down), "wide", 1)
        grad1 = [after(grad1[0], gate_near, d_down), *grad1[1:]]
        grad_attended = out_back(grad1, attn, s.qkv, s.heads)
        if layer == 0:
            crossed = [partner_one(x, 0) for x in after(tuple(terms[1]), grad_attended)]
        else:
            given1 = give(after(out1, grad_attended), 1)
        back = lambda m, grad, before: attend_back(
            m, q, grad, attended, lse, kv, tables[0], tables[1], loc, pos, before
        )
        grad_attended = grad_attended.reshape(q.shape)
        dq, send0, keep0 = back(0, grad_attended, q)
        got0 = partner(halved(send0), "wide", 1)
        if layer == 0:
            down_crossed = partner_one(after(d_down, send0), 1)
        dq, send1_, keep1 = back(1, after(grad_attended, send0), dq)
        if layer == 0:
            dq, down_crossed = lax.optimization_barrier((dq, down_crossed))
        up_got, got0, d_gate = after((up_got, got0, d_gate), dq)
        near0 = reduce_near(halved(keep0), got0)
        if layer == 0:
            gate_crossed = partner_one(after(d_gate, near0), 1)
        got1 = partner(after(halved(send1_), near0), "wide", 1)
        dkv0 = reduce_far(near0)
        up_near = near_sum(up_keep, after(up_got, near0))
        d_up = reduce_line(up_near)
        out_send, out_keep = weight_grad(
            [after(x, up_near, d_gate) for x in grad1], [flat], count
        )
        if layer:
            out_send, given1 = lax.optimization_barrier((out_send, given1))
            section_out = jnp.where(home, given0, given1)
        dkv1 = reduce_far(reduce_near(halved(keep1), after(got1, out_send)))
        if layer == 0:
            crossed = list(after(tuple(crossed), dq))
            dkv1 = after(dkv1, *crossed)
        half = HD // 2
        back_rows = []
        for dkv in (dkv0, dkv1):
            turned = jnp.concatenate(
                [dkv[..., half:HD], dkv[..., :half], jnp.zeros_like(dkv[..., HD:])], axis=-1
            )
            back_rows.append(dkv * by_piece(tables[2]) - turned * by_piece(tables[3]))
        dkv = jnp.stack(back_rows, axis=1).astype(BF)
        dq, dkv = after(dq, out_send).reshape(-1, s.heads), dkv.reshape(-1, PAIR)
        if layer == 0:
            out_got = partner(after(out_send, got1), "wide", 1)
            dkv, gate_crossed = lax.optimization_barrier((dkv, gate_crossed))
            crossed_0 = [gate_crossed, down_crossed]
        own, send = contract([dq, dkv], [(attn,), (attn,)], (0, s.heads), s.depth, s.width)
        if layer == 0:
            out_near = near_sum(out_keep, after(out_got, own))
            d_out = reduce_line(out_near)
            own = after(own, out_near)
        qkv_send, qkv_keep = weight_grad(
            [after(x, own) for x in normed], [dq, dkv], count
        )
        if layer:
            pack_got = partner(
                jnp.concatenate([after(qkv_send, dkv1), out_send], axis=2), "wide", 1
            )
            grad2, _, first_gain, _ = exchange(
                after(own, qkv_send),
                send,
                grad_middle,
                gains[0],
                u,
                first_scale,
                keep_f32=False,
                ident=3,
            )
            grads[1] = upstream = grad2[0]
            grads_out = give(upstream, 1)
            pack_got, d_up = after((pack_got, d_up), grad2[0])
            pack_near = near_sum(jnp.concatenate([qkv_keep, out_keep], axis=2), pack_got)
            d_attn = reduce_line(after(pack_near, d_up))
            grad2 = [after(x, pack_near) for x in grad2]
            terms[1] = [None, d_gate, d_up, d_down]
        else:
            grads[0], _, first_gain, got = exchange(
                own,
                send,
                grad_middle,
                gains[0],
                u,
                first_scale,
                keep_f32=False,
                last=True,
                bulk=(qkv_send,),
                ident=4,
            )
            grads[0] = grads[0][0]
            qkv_near = near_sum(qkv_keep, got[0])
            blocks = qkv_near.reshape(count // 2, s.depth, -1)
            d_qkv = blocks[wide // 2].astype(F32)
            for j in range(1, count // 2):
                block = partner(blocks[(wide // 2) ^ j], "wide", 2 * j)
                d_qkv = d_qkv + block.astype(F32)
            d_qkv = d_qkv.astype(BF)
            terms[0] = [d_qkv, d_out, d_gate, d_up, d_down]
        gain_terms += [first_gain.reshape(1, -1), second_gain.reshape(1, -1)]

    given = (give(grads[0], 0), grads_out)
    up_crossed = partner_one(after(d_up, grads[0]), 1)
    d_qkv_out, *given = lax.optimization_barrier((d_qkv, *given))
    input_grads = jnp.where(home, *given)
    late = [partner_one(x, 1) for x in (d_qkv_out, d_out)]
    crossed_0 = [*late, crossed_0[0], up_crossed, crossed_0[1]]
    crossed = [crossed[0][:, : s.qkv], crossed[0][:, s.qkv :], *crossed[1:]]
    terms[1] = [terms[1][0][:, : s.qkv], terms[1][0][:, s.qkv :], *terms[1][1:]]
    gain_total = jnp.concatenate(gain_terms, axis=0)
    gain_total = gain_total + partner(gain_total, "tp", 1)
    gain_total = gain_total + partner(gain_total, "section", 1)
    gain_total = gain_total.reshape(4, count // 2, 2, s.depth)
    gain_total = gain_total[:, :, side()] + partner(gain_total[:, :, 1 - side()], "wide", 1)
    total = gain_total[:, wide // 2]
    for j in range(1, count // 2):
        total = total + partner(gain_total[:, (wide // 2) ^ j], "wide", 2 * j)
    gain_total = total
    gains = jnp.where(home, gain_total[2:], gain_total[:2])

    def settle(index):
        own = jnp.where(home, terms[0][index], terms[1][index]).astype(F32)
        other = crossed[index].astype(F32) + crossed_0[index].astype(F32)
        return jnp.where(home, own, other), jnp.where(home, other, own)

    heads = s.heads
    low, high = settle(0)
    cut = lambda start, size: jnp.concatenate(
        [low[:, start : start + size], high[:, start : start + size]], axis=1
    )
    d_query = cut(0, heads)
    d_key = cut(heads, HD)
    d_value = cut(heads + HD, HD)
    d_out = jnp.concatenate([half.T for half in settle(1)], axis=0)
    d_gate = jnp.concatenate(settle(2), axis=1)
    d_up = jnp.concatenate(settle(3), axis=1)
    d_down = jnp.concatenate([half.T for half in settle(4)], axis=0)
    return (
        section_out[None],
        input_grads[None],
        gains[0:1],
        d_query[None],
        d_key[None],
        d_value[None],
        d_out[None],
        gains[1:2],
        d_gate[None],
        d_up[None],
        d_down[None],
    )


def solution(mesh):
    return jax.shard_map(
        shards,
        mesh=mesh,
        in_specs=(
            P(None, ("wide", "tp"), None),
            P(None, ("wide", "tp"), None),
            P("section", "wide"),
            P("section", "wide", "tp"),
            P("section", "wide", "tp"),
            P("section", "wide", "tp"),
            P("section", "tp", "wide"),
            P("section", "wide"),
            P("section", "wide", "tp"),
            P("section", "wide", "tp"),
            P("section", "tp", "wide"),
        ),
        out_specs=(
            P("section", None, ("wide", "tp"), None),
            P("section", None, ("wide", "tp"), None),
            P("section", "wide"),
            P("section", "wide", "tp"),
            P("section", "wide", "tp"),
            P("section", "wide", "tp"),
            P("section", "tp", "wide"),
            P("section", "wide"),
            P("section", "wide", "tp"),
            P("section", "wide", "tp"),
            P("section", "tp", "wide"),
        ),
        check_vma=False,
    )
```

```python
import functools
import math

import jax
import jax.numpy as jnp
from jax import lax
from jax.experimental import pallas as pl
from jax.experimental.pallas import tpu as pltpu
from jax.sharding import PartitionSpec as P

HD = 64
PAIR = 2 * HD
EPSILON = 1e-05
GAIN_ROWS = 16
VMEM = 48 * 2**20
BF = jnp.bfloat16
F32 = jnp.float32
ANY = pl.BlockSpec(memory_space=pl.ANY)


def partner(x, axis, bit):
    peers = lax.axis_size(axis)
    return lax.ppermute(x, axis, [(i, i ^ bit) for i in range(peers)])


def partner_one(x, source):
    return lax.ppermute(x, "section", [(source, 1 - source)])


def after(value, *events):
    return lax.optimization_barrier((value,) + events)[0]


def product(left, right):
    return jnp.dot(left, right, preferred_element_type=F32)


def cross(left, right):
    return lax.dot_general(left, right, (((0,), (0,)), ((), ())), preferred_element_type=F32)


def against(left, right):
    return lax.dot_general(left, right, (((1,), (1,)), ((), ())), preferred_element_type=F32)


def call(body, ins, outs, scratch, flops, exps=0, ident=None, light=False, **more):
    moved = sum(x.size * x.dtype.itemsize for x in list(ins) + list(outs))
    if light:
        moved, flops, exps = moved // 8, flops // 8, exps // 8
    remote = {} if ident is None else {"collective_id": ident, "has_side_effects": True}
    return pl.pallas_call(
        body,
        out_shape=outs,
        scratch_shapes=scratch,
        compiler_params=pltpu.CompilerParams(vmem_limit_bytes=VMEM, **remote),
        cost_estimate=pl.CostEstimate(
            flops=int(flops), bytes_accessed=int(moved), transcendentals=int(exps)
        ),
        **more,
    )(*ins)


def shaped(*dims, kind=BF):
    return jax.ShapeDtypeStruct(dims, kind)


def lines():
    count = lax.axis_size("wide")
    return [list(range(y, count, 2)) for y in range(2)]


def side():
    return lax.axis_index("wide") % 2


def gather_line(shard):
    return lax.all_gather(shard, "wide", axis=0, tiled=True, axis_index_groups=lines())


def reduce_line(near):
    return lax.psum_scatter(
        near, "wide", scatter_dimension=0, tiled=True, axis_index_groups=lines()
    )


def gather_blocks(shard):
    count = lax.axis_size("wide")
    far = [shard if k == 0 else partner(shard, "wide", k) for k in range(0, count, 2)]
    blocks = []
    for block in far:
        blocks += [block, partner(block, "wide", 1)]
    return blocks


def reduce_near(keep, got):
    return keep.astype(F32) + got.astype(F32)


def reduce_far(near):
    total = near[0]
    for j in range(1, near.shape[0]):
        total = total + partner(near[j].astype(BF), "wide", 2 * j).astype(F32)
    return total


def mirror(x, cross=0, sections=(0, 1)):
    count = lax.axis_size("wide")
    pairs = []
    for section in sections:
        for w in range(count):
            for core in range(2):
                to = w if core == 0 else count - 1 - w
                pairs.append(
                    ((section * count + w) * 2 + core, ((section ^ cross) * count + to) * 2 + core)
                )
    return lax.ppermute(x, ("section", "wide", "tp"), pairs)


def spread(values):
    other = partner(values, "section", 1)
    return [values, other, partner(values, "tp", 1), partner(other, "tp", 1)]


def fold(own, send):
    rows = own.shape[0] // 2
    got = partner(send, "tp", 1)
    away = (own[rows:].astype(F32) + got[rows:].astype(F32)).astype(BF)
    mine = own[:rows].astype(F32) + got[:rows].astype(F32)
    return mine + partner(away, "section", 1).astype(F32)


def load_attn(ref, dest, sem, start):
    copy = pltpu.make_async_copy(ref.at[:, pl.ds(start, dest.shape[1])], dest, sem.at[0])
    copy.start()
    return [copy]


def load_sides(refs, dest, sem, depth, first=0):
    copies = []
    if len(refs) == 1:
        copies.append(pltpu.make_async_copy(refs[0], dest, sem.at[first]))
        copies[-1].start()
        return copies
    y = side()
    for s, ref in enumerate(refs):
        for j in range(dest.shape[0] // (2 * depth)):
            place = pl.multiple_of((2 * j + (y + s) % 2) * depth, depth)
            copies.append(
                pltpu.make_async_copy(
                    ref.at[pl.ds(j * depth, depth)],
                    dest.at[pl.ds(place, depth)],
                    sem.at[first + 2 * j + s],
                )
            )
            copies[-1].start()
    return copies


def exchange_kernel(back, keep_f32, last, bulk, *refs):
    own_ref, send_ref, base_ref, gain_ref = refs[:4]
    refs = refs[4:]
    if back:
        values_ref, scale_ref = refs[:2]
        refs = refs[2:]
    bulk_in, refs = refs[:bulk], refs[bulk:]
    held = 1 if last else 4
    pieces, refs = refs[:held], refs[held:]
    first_out, second_out = refs[:2]
    bulk_out, refs = refs[2 : 2 + bulk], refs[2 + bulk :]
    got_tp, away, got_section, low, send_sem, recv_sem, local_sem, bulk_sem = refs
    rows, width = low.shape
    chunks = 4
    size = rows // chunks
    peers = {
        "tp": {"tp": 1 - lax.axis_index("tp")},
        "section": {"section": 1 - lax.axis_index("section")},
        "near": {"wide": lax.axis_index("wide") + 1 - 2 * side()},
    }
    greeted = ["tp", "section"] + (["near"] if bulk else [])
    barrier = pltpu.get_barrier_semaphore()
    for name in greeted:
        pl.semaphore_signal(
            barrier, inc=1, device_id=peers[name], device_id_type=pl.DeviceIdType.MESH
        )
    pl.semaphore_wait(barrier, len(greeted))

    def remote(source, target, index, name):
        copy = pltpu.make_async_remote_copy(
            src_ref=source,
            dst_ref=target,
            send_sem=send_sem.at[index],
            recv_sem=recv_sem.at[index],
            device_id=peers[name],
            device_id_type=pl.DeviceIdType.MESH,
        )
        copy.start()
        return copy

    bulk_copies = [
        pltpu.make_async_remote_copy(
            src_ref=bulk_in[i],
            dst_ref=bulk_out[i],
            send_sem=bulk_sem.at[0, i],
            recv_sem=bulk_sem.at[1, i],
            device_id=peers["near"],
            device_id_type=pl.DeviceIdType.MESH,
        )
        for i in range(bulk)
    ]
    for copy in bulk_copies:
        copy.start()
    span = lambda c: pl.ds(c * size, size)
    sums = [
        remote(send_ref.at[pl.ds(rows, rows)], got_tp.at[1], 0, "tp"),
        remote(send_ref.at[pl.ds(0, rows)], got_tp.at[0], 1, "tp"),
    ]
    sums[0].wait()
    crossing = []
    for c in range(chunks):
        total = own_ref[rows + c * size : rows + (c + 1) * size].astype(F32)
        away[span(c)] = (total + got_tp[1, span(c)].astype(F32)).astype(BF)
        crossing.append(remote(away.at[span(c)], got_section.at[span(c)], 2 + c, "section"))
    sums[1].wait()
    over_section, over_tp, local = [], [], []
    gain = gain_ref[...]
    gain_total = jnp.zeros((1, width), F32)
    for c in range(chunks):
        here = slice(c * size, (c + 1) * size)
        crossing[c].wait()
        total = own_ref[here].astype(F32) + got_tp[0, here].astype(F32)
        total = total + got_section[here].astype(F32)
        base = base_ref[here].astype(F32)
        if back:
            scale = scale_ref[here]
            norm = values_ref[here].astype(F32) * scale
            scaled = total * gain
            mean = jnp.mean(scaled * norm, axis=-1, keepdims=True)
            gain_total = gain_total + jnp.sum(total * norm, axis=0, keepdims=True)
            result = base + scale * (scaled - norm * mean)
            if keep_f32:
                first_out[here] = result
            low[here] = result.astype(BF)
        else:
            result = base + total
            if keep_f32:
                first_out[here] = result
            else:
                first_out[here] = result.astype(BF)
                result = result.astype(BF).astype(F32)
            scale = lax.rsqrt(jnp.mean(result * result, axis=-1, keepdims=True) + EPSILON)
            second_out[here] = scale
            low[here] = (result * scale * gain).astype(BF)
        copy = pltpu.make_async_copy(low.at[span(c)], pieces[0].at[span(c)], local_sem.at[c])
        copy.start()
        local.append(copy)
        if last:
            continue
        over_section.append(
            remote(low.at[span(c)], pieces[1].at[span(c)], 2 + chunks + c, "section")
        )
        over_tp.append(remote(low.at[span(c)], pieces[2].at[span(c)], 2 + 2 * chunks + c, "tp"))
    if back:
        second_out[...] = gain_total
        if not keep_f32:
            first_out[...] = gain_total
    forwarded = []
    for c in range(0 if last else chunks):
        over_section[c].wait()
        forwarded.append(
            remote(pieces[1].at[span(c)], pieces[3].at[span(c)], 2 + 3 * chunks + c, "tp")
        )
    for copy in local + over_tp + forwarded + bulk_copies:
        copy.wait()


def exchange(
    own, send, base, gain, values=None, scale=None, keep_f32=True, last=False, bulk=(), ident=0
):
    rows, width = base.shape
    back = values is not None
    vmem = pl.BlockSpec(memory_space=pltpu.VMEM)
    ins = [own, send, base, gain.reshape(1, width)] + ([values, scale] if back else [])
    piece = shaped(rows, width)
    if back:
        first = shaped(rows, width, kind=F32) if keep_f32 else shaped(1, width, kind=F32)
        second = shaped(1, width, kind=F32)
    else:
        first = shaped(rows, width, kind=F32 if keep_f32 else BF)
        second = shaped(rows, 1, kind=F32)
    count = 2 + 4 * 4
    held = 1 if last else 4
    outs = call(
        functools.partial(exchange_kernel, back, keep_f32, last, len(bulk)),
        [*ins, *bulk],
        [piece] * held + [first, second] + [shaped(*x.shape) for x in bulk],
        [
            pltpu.VMEM((2, rows, width), BF),
            pltpu.VMEM((rows, width), BF),
            pltpu.VMEM((rows, width), BF),
            pltpu.VMEM((rows, width), BF),
            pltpu.SemaphoreType.DMA((count,)),
            pltpu.SemaphoreType.DMA((count,)),
            pltpu.SemaphoreType.DMA((4,)),
            pltpu.SemaphoreType.DMA((2, max(1, len(bulk)))),
        ],
        60e9,
        ident=ident,
        light=back,
        in_specs=[vmem] * len(ins) + [ANY] * len(bulk),
        out_specs=[ANY] * held + [vmem] * 2 + [ANY] * len(bulk),
    )
    return outs[:held], outs[held], outs[held + 1], outs[held + 2 :]


def qkv_kernel(*refs):
    pieces, attn, tables = refs[:4], refs[4], refs[5:9]
    q_ref, kv_ref, w, sem = refs[9:]
    width = w.shape[1]
    for copy in load_attn(attn, w, sem, 0):
        copy.wait()
    cos, sin, cos_kv, sin_kv = tables
    for p, piece in enumerate(pieces):
        linear = product(piece[...], w[...])
        micro, rows = q_ref.shape[1], q_ref.shape[2]
        first = lax.broadcasted_iota(jnp.int32, (rows, PAIR), 1) % HD < HD // 2
        span = slice(p * rows, (p + 1) * rows)
        for m in range(micro):
            for start in range(0, width, PAIR):
                part = linear[m * rows : (m + 1) * rows, start : start + PAIR]
                turned = jnp.where(
                    first, pltpu.roll(part, PAIR - HD // 2, 1), pltpu.roll(part, HD // 2, 1)
                )
                if start + PAIR < width:
                    out = part * cos[span] + turned * sin[span]
                    q_ref[p, m, :, start : start + PAIR] = out.astype(BF)
                else:
                    out = part * cos_kv[span] + turned * sin_kv[span]
                    kv_ref[p, m] = out.astype(BF)


def qkv_project(pieces, attn, tables, micro, width):
    total, d = pieces[0].shape
    rows = total // micro
    vmem = pl.BlockSpec(memory_space=pltpu.VMEM)
    return call(
        qkv_kernel,
        [*pieces, attn, *tables],
        [shaped(4, micro, rows, width - PAIR), shaped(4, micro, rows, PAIR)],
        [pltpu.VMEM((d, width), BF), pltpu.SemaphoreType.DMA((1,))],
        8 * total * d * width,
        in_specs=[vmem] * 4 + [ANY] + [vmem] * 4,
        out_specs=[vmem] * 2,
    )


def gate_up_kernel(depth, sides, *refs):
    pieces, refs = refs[:4], refs[4:]
    gates, ups, refs = refs[: sides[0]], refs[sides[0] : sum(sides)], refs[sum(sides) :]
    outs = refs[:3]
    x, w_gate, w_up, buffer, x_sem, w_sem, out_sem = refs[3:]
    copies = load_sides(gates, w_gate, w_sem, depth)
    copies += load_sides(ups, w_up, w_sem, depth, w_gate.shape[0] // depth)
    inputs = []
    for p, piece in enumerate(pieces):
        inputs.append(pltpu.make_async_copy(piece, x.at[p], x_sem.at[p]))
        inputs[-1].start()
    for copy in copies:
        copy.wait()
    rows = x.shape[1]
    results = []
    for p in range(4):
        inputs[p].wait()
        gate = product(x[p], w_gate[...])
        up = product(x[p], w_up[...])
        if p >= 2:
            for copy in results[p - 2]:
                copy.wait()
        slot = p % 2
        buffer[slot, 0] = gate.astype(BF)
        buffer[slot, 1] = up.astype(BF)
        buffer[slot, 2] = (gate * jax.nn.sigmoid(gate) * up).astype(BF)
        results.append(
            [
                pltpu.make_async_copy(
                    buffer.at[slot, i], outs[i].at[pl.ds(p * rows, rows)], out_sem.at[p, i]
                )
                for i in range(3)
            ]
        )
        for copy in results[p]:
            copy.start()
    for p in (2, 3):
        for copy in results[p]:
            copy.wait()


def gate_up(pieces, gates, ups, depth):
    rows, d = pieces[0].shape
    hidden = gates[0].shape[1]
    return call(
        functools.partial(gate_up_kernel, depth, (len(gates), len(ups))),
        [*pieces, *gates, *ups],
        [shaped(4 * rows, hidden)] * 3,
        [
            pltpu.VMEM((4, rows, d), BF),
            pltpu.VMEM((d, hidden), BF),
            pltpu.VMEM((d, hidden), BF),
            pltpu.VMEM((2, 3, rows, hidden), BF),
            pltpu.SemaphoreType.DMA((4,)),
            pltpu.SemaphoreType.DMA((2 * d // depth,)),
            pltpu.SemaphoreType.DMA((4, 3)),
        ],
        16 * rows * d * hidden,
        4 * rows * hidden,
        in_specs=[ANY] * (4 + len(gates) + len(ups)),
        out_specs=[ANY] * 3,
    )


def hidden_back_kernel(depth, *refs):
    pieces, downs = refs[:4], refs[4:6]
    gate_ref, up_ref = refs[6:8]
    outs = refs[8:10]
    x, w, kept, buffer, x_sem, w_sem, kept_sem, out_sem = refs[10:]
    copies = load_sides(downs, w, w_sem, depth)
    rows = x.shape[1]
    inputs = []
    for p, piece in enumerate(pieces):
        span = pl.ds(p * rows, rows)
        inputs.append(
            [
                pltpu.make_async_copy(piece, x.at[p], x_sem.at[p]),
                pltpu.make_async_copy(gate_ref.at[span], kept.at[p, 0], kept_sem.at[p, 0]),
                pltpu.make_async_copy(up_ref.at[span], kept.at[p, 1], kept_sem.at[p, 1]),
            ]
        )
        for copy in inputs[-1]:
            copy.start()
    for copy in copies:
        copy.wait()
    results = []
    for p in range(4):
        for copy in inputs[p]:
            copy.wait()
        grad = product(x[p], w[...])
        gate = kept[p, 0].astype(F32)
        up = kept[p, 1].astype(F32)
        sigma = jax.nn.sigmoid(gate)
        if p >= 2:
            for copy in results[p - 2]:
                copy.wait()
        slot = p % 2
        buffer[slot, 0] = (grad * up * sigma * (1.0 + gate * (1.0 - sigma))).astype(BF)
        buffer[slot, 1] = (grad * gate * sigma).astype(BF)
        results.append(
            [
                pltpu.make_async_copy(
                    buffer.at[slot, i], outs[i].at[pl.ds(p * rows, rows)], out_sem.at[p, i]
                )
                for i in range(2)
            ]
        )
        for copy in results[p]:
            copy.start()
    for p in (2, 3):
        for copy in results[p]:
            copy.wait()


def hidden_back(pieces, downs, gate, up, depth):
    rows, d = pieces[0].shape
    hidden = downs[0].shape[1]
    return call(
        functools.partial(hidden_back_kernel, depth),
        [*pieces, *downs, gate, up],
        [shaped(4 * rows, hidden)] * 2,
        [
            pltpu.VMEM((4, rows, d), BF),
            pltpu.VMEM((d, hidden), BF),
            pltpu.VMEM((4, 2, rows, hidden), BF),
            pltpu.VMEM((2, 2, rows, hidden), BF),
            pltpu.SemaphoreType.DMA((4,)),
            pltpu.SemaphoreType.DMA((d // depth,)),
            pltpu.SemaphoreType.DMA((4, 2)),
            pltpu.SemaphoreType.DMA((4, 2)),
        ],
        8 * rows * d * hidden,
        4 * rows * hidden,
        in_specs=[ANY] * 8,
        out_specs=[ANY] * 2,
        light=True,
    )


def out_back_kernel(offset, *refs):
    pieces, attn = refs[:4], refs[4]
    out_ref, w, sem = refs[5:]
    for copy in load_attn(attn, w, sem, offset):
        copy.wait()
    rows = pieces[0].shape[0]
    for p, piece in enumerate(pieces):
        out_ref[p * rows : (p + 1) * rows] = product(piece[...], w[...]).astype(BF)


def out_back(pieces, attn, offset, width):
    rows, d = pieces[0].shape
    vmem = pl.BlockSpec(memory_space=pltpu.VMEM)
    return call(
        functools.partial(out_back_kernel, offset),
        [*pieces, attn],
        [shaped(4 * rows, width)],
        [pltpu.VMEM((d, width), BF), pltpu.SemaphoreType.DMA((1,))],
        8 * rows * d * width,
        in_specs=[vmem] * 4 + [ANY],
        out_specs=[vmem],
        light=True,
    )[0]


def contract_kernel(depth, starts, sizes, *refs):
    sides = len(starts)
    lefts, refs = refs[:sides], refs[sides:]
    sources = []
    for size in sizes:
        sources.append(refs[:size])
        refs = refs[size:]
    own_ref, send_ref = refs[:2]
    weights, sem = refs[2:-1], refs[-1]
    step = pl.program_id(0)
    half = pl.num_programs(0) // 2

    @pl.when(step == 0)
    def _():
        copies = []
        for s, start in enumerate(starts):
            if start is None:
                copies += load_sides(sources[s], weights[s], sem.at[s], depth)
            else:
                copies += load_attn(sources[s][0], weights[s], sem.at[s], start)
        for copy in copies:
            copy.wait()

    total = against(lefts[0][...], weights[0][...])
    for s in range(1, sides):
        total = total + against(lefts[s][...], weights[s][...])
    total = total.astype(BF)

    @pl.when(step < half)
    def _():
        send_ref[...] = total

    @pl.when(step >= half)
    def _():
        own_ref[...] = total


def contract(lefts, sources, starts, depth, width):
    sides = len(lefts)
    total = lefts[0].shape[0]
    tile = total // 4
    flat = [ref for group in sources for ref in group]
    return call(
        functools.partial(contract_kernel, depth, starts, [len(group) for group in sources]),
        [*lefts, *flat],
        [shaped(total // 2, width)] * 2,
        [pltpu.VMEM((width, left.shape[1]), BF) for left in lefts]
        + [pltpu.SemaphoreType.DMA((sides, width // depth))],
        sum(2 * total * left.shape[1] * width for left in lefts),
        grid=(4,),
        in_specs=[
            pl.BlockSpec((tile, left.shape[1]), lambda i: ((i + 2) % 4, 0)) for left in lefts
        ]
        + [ANY] * len(flat),
        out_specs=[
            pl.BlockSpec((tile, width), lambda i: (jnp.maximum(i - 2, 0), 0)),
            pl.BlockSpec((tile, width), lambda i: (jnp.minimum(i, 1), 0)),
        ],
    )


def weight_kernel(rights, split, *refs):
    pieces, right_refs, outs = refs[:4], refs[4 : 4 + rights], refs[4 + rights :]
    left = jnp.concatenate([x[...] for x in pieces], axis=0)
    start = 0
    for right in right_refs:
        grad = cross(left, right[...]).astype(BF)
        span = slice(start, start + right.shape[1])
        start += right.shape[1]
        if not split:
            outs[0][:, span] = grad
            continue
        send_ref, keep_ref = outs
        depth = keep_ref.shape[1]
        for y, (first, second) in enumerate(((keep_ref, send_ref), (send_ref, keep_ref))):

            @pl.when(side() == y)
            def _():
                first[0, :, span] = grad[:depth]
                second[0, :, span] = grad[depth:]


def weight_grad(pieces, rights, n, split=True):
    rows, d = pieces[0].shape
    width = sum(right.shape[1] for right in rights)
    depth = d // n
    if split:
        shapes = [shaped(n // 2, depth, width)] * 2
        specs = [pl.BlockSpec((1, depth, width), lambda j: (j, 0, 0))] * 2
    else:
        shapes = [shaped(d, width)]
        specs = [pl.BlockSpec((2 * depth, width), lambda j: (j, 0))]
    outs = call(
        functools.partial(weight_kernel, len(rights), split),
        [*pieces, *rights],
        shapes,
        [],
        8 * rows * d * width,
        grid=(n // 2,),
        in_specs=[pl.BlockSpec((rows, 2 * depth), lambda j: (0, j))] * 4
        + [pl.BlockSpec(right.shape, lambda j: (0, 0)) for right in rights],
        out_specs=specs,
        light=True,
    )
    return outs if split else outs[0]


def stack_heads(x):
    return jnp.concatenate([x[:, h : h + HD] for h in range(0, x.shape[1], HD)], axis=0)


def turn_heads(x):
    pairs = [x[:, g : g + PAIR].T for g in range(0, x.shape[1], PAIR)]
    return jnp.concatenate([part for pair in pairs for part in (pair[:HD], pair[HD:])], axis=1)


def back_heads(x, rows, g):
    even = x[:, 2 * g * rows : (2 * g + 1) * rows]
    odd = x[:, (2 * g + 1) * rows : (2 * g + 2) * rows]
    return jnp.concatenate([even, odd], axis=0).T


def attend_kernel(
    block, loc_ref, pos_ref, q_ref, kv_ref, o_ref, lse_ref, k_ref, vt_ref, m_ref, acc_ref, s_ref
):
    piece = pl.program_id(1)
    rows = q_ref.shape[2]
    count = kv_ref.shape[0]
    per_block = block // rows

    @pl.when(piece == 0)
    def _():
        def one(i, _):
            kv = kv_ref[loc_ref[i], 0]
            k_ref[i] = kv[:, :HD]
            ones = jnp.ones((GAIN_ROWS, rows), BF)
            vt_ref[i] = jnp.concatenate([kv.T[HD:], ones], axis=0)
            return 0

        lax.fori_loop(0, count, one, 0)

    pos = pos_ref[piece]
    queries = turn_heads(q_ref[0, 0] * BF(1.0 / math.sqrt(HD)))
    m_ref[...] = jnp.full(m_ref.shape, -1e30, F32)
    acc_ref[...] = jnp.zeros(acc_ref.shape, F32)

    def scores_of(j):
        first = j * per_block
        keys = jnp.concatenate([k_ref[first + i] for i in range(per_block)], axis=0)
        return product(keys, queries)

    def absorb(j, scores):
        first = j * per_block
        used = scores.shape[0] // rows
        values = jnp.concatenate([vt_ref[first + i] for i in range(used)], axis=1)
        before = m_ref[...]
        now = jnp.maximum(before, jnp.max(scores, axis=0, keepdims=True))
        terms = jnp.exp(scores - now)
        shrink = jnp.exp(before - now)
        acc_ref[...] = acc_ref[...] * shrink + product(values, terms.astype(BF))
        m_ref[...] = now

    full = pos // block
    s_ref[0] = scores_of(0)

    def loop(j, _):
        slot = j % 2
        following = scores_of(j + 1)
        absorb(j, s_ref[slot])
        s_ref[1 - slot] = following
        return 0

    lax.fori_loop(0, full, loop, 0)

    def diagonal(size):
        scores = s_ref[full % 2, :size]
        row = lax.broadcasted_iota(jnp.int32, scores.shape, 0)
        column = lax.broadcasted_iota(jnp.int32, scores.shape, 1) % rows
        absorb(full, jnp.where(row + full * block <= column + pos, scores, -1e30))

    half = pos - full * block < block // 2

    @pl.when(half)
    def _():
        diagonal(block // 2)

    @pl.when(jnp.logical_not(half))
    def _():
        diagonal(block)

    total = acc_ref[HD : HD + 1]
    out = acc_ref[:HD] / total
    lse_ref[0, 0] = m_ref[...] + jnp.log(total)
    for g in range(q_ref.shape[3] // PAIR):
        o_ref[0, 0, :, g * PAIR : (g + 1) * PAIR] = back_heads(out, rows, g).astype(BF)


def attend(q, kv, loc, pos):
    pieces, micro, rows, width = q.shape
    count = kv.shape[0]
    stacked = rows * width // HD
    block = min(512, rows * count)
    scores = micro * pieces * stacked * rows * count // 2
    heads = pl.BlockSpec((1, 1, rows, width), lambda m, p, *_: (p, m, 0, 0))
    return call(
        functools.partial(attend_kernel, block),
        [loc, pos, q, kv],
        [shaped(*q.shape), shaped(pieces, micro, 1, stacked, kind=F32)],
        (),
        scores * 2750,
        scores,
        grid_spec=pltpu.PrefetchScalarGridSpec(
            num_scalar_prefetch=2,
            grid=(micro, pieces),
            in_specs=[
                heads,
                pl.BlockSpec((count, 1, rows, PAIR), lambda m, p, *_: (0, m, 0, 0)),
            ],
            out_specs=[
                heads,
                pl.BlockSpec((1, 1, 1, stacked), lambda m, p, *_: (p, m, 0, 0)),
            ],
            scratch_shapes=[
                pltpu.VMEM((count, rows, HD), BF),
                pltpu.VMEM((count, HD + GAIN_ROWS, rows), BF),
                pltpu.VMEM((1, stacked), F32),
                pltpu.VMEM((HD + GAIN_ROWS, stacked), F32),
                pltpu.VMEM((2, block, stacked), F32),
            ],
        ),
    )


def attend_back_kernel(
    block,
    loc_ref,
    pos_ref,
    q_ref,
    do_ref,
    o_ref,
    lse_ref,
    kv_ref,
    cos_ref,
    sin_ref,
    before_ref,
    dq_ref,
    send_ref,
    keep_ref,
    k_ref,
    v_ref,
    kt_ref,
    dq_acc,
    dk_acc,
    dv_acc,
):
    piece = pl.program_id(0)
    rows = q_ref.shape[2]
    count = kv_ref.shape[0]
    per_block = block // rows
    scale = 1.0 / math.sqrt(HD)

    @pl.when(piece == 0)
    def _():
        def one(i, _):
            kv = kv_ref[loc_ref[i], 0]
            k_ref[i] = kv[:, :HD]
            v_ref[i] = kv[:, HD:]
            kt_ref[i] = kv.T[:HD]
            dk_acc[i] = jnp.zeros(dk_acc.shape[1:], F32)
            dv_acc[i] = jnp.zeros(dv_acc.shape[1:], F32)
            return 0

        lax.fori_loop(0, count, one, 0)

    pos = pos_ref[piece]
    q = q_ref[0, 0] * BF(scale)
    do = do_ref[0, 0]
    queries, queries_t = stack_heads(q), turn_heads(q)
    grads, grads_t = stack_heads(do), turn_heads(do)
    dots = turn_heads(do.astype(F32) * o_ref[0, 0].astype(F32))
    delta = jnp.sum(dots, axis=0, keepdims=True)
    logs = lse_ref[0, 0]
    dq_acc[...] = jnp.zeros(dq_acc.shape, F32)

    def step(j, masked, used=per_block):
        first = j * per_block
        keys = jnp.concatenate([k_ref[first + i] for i in range(used)], axis=0)
        values = jnp.concatenate([v_ref[first + i] for i in range(used)], axis=0)
        keys_t = jnp.concatenate([kt_ref[first + i] for i in range(used)], axis=1)
        scores = product(keys, queries_t)
        probs = jnp.exp(scores - logs)
        if masked:
            row = lax.broadcasted_iota(jnp.int32, scores.shape, 0)
            column = lax.broadcasted_iota(jnp.int32, scores.shape, 1) % rows
            probs = jnp.where(row + j * block <= column + pos, probs, 0.0)
        grad_probs = product(values, grads_t)
        grad_low = (probs * (grad_probs - delta)).astype(BF)
        dv = product(probs.astype(BF), grads)
        dk = product(grad_low, queries)
        dq_acc[...] += product(keys_t, grad_low)
        for i in range(used):
            dk_acc[first + i] += dk[i * rows : (i + 1) * rows]
            dv_acc[first + i] += dv[i * rows : (i + 1) * rows]

    full = pos // block

    def loop(j, _):
        step(j, False)
        return 0

    lax.fori_loop(0, full, loop, 0)
    half = pos - full * block < block // 2

    @pl.when(half)
    def _():
        step(full, True, per_block // 2)

    @pl.when(jnp.logical_not(half))
    def _():
        step(full, True)

    first = lax.broadcasted_iota(jnp.int32, (rows, PAIR), 1) % HD < HD // 2
    for g in range(q_ref.shape[3] // PAIR):
        part = back_heads(dq_acc[...], rows, g) * scale
        turned = jnp.where(
            first, pltpu.roll(part, PAIR - HD // 2, 1), pltpu.roll(part, HD // 2, 1)
        )
        out = part * cos_ref[...] - turned * sin_ref[...]
        dq_ref[0, 0, :, g * PAIR : (g + 1) * PAIR] = out.astype(BF)

    @pl.when(piece == pl.num_programs(0) - 1)
    def _():
        pieces = pl.num_programs(0)

        def one(i, _):
            grad = jnp.concatenate([dk_acc[i], dv_acc[i]], axis=1).astype(BF)
            place = loc_ref[i]
            owner = place // pieces
            slot = owner // 2 * pieces + place % pieces

            @pl.when(owner % 2 == 0)
            def _():
                keep_ref[slot] = grad

            @pl.when(owner % 2 == 1)
            def _():
                send_ref[slot] = grad

            return 0

        lax.fori_loop(0, count, one, 0)


def attend_back(m, q, grad, attended, lse, kv, cos, sin, loc, pos, before):
    pieces, micro, rows, width = q.shape
    count = kv.shape[0]
    stacked = rows * width // HD
    block = min(512, rows * count)
    scores = pieces * stacked * rows * count // 2
    heads = pl.BlockSpec((1, 1, rows, width), lambda p, *_: (p, m, 0, 0))
    half = pl.BlockSpec((count // 2, rows, PAIR), lambda p, *_: (0, 0, 0))
    table = pl.BlockSpec((rows, PAIR), lambda p, *_: (p, 0))
    return call(
        functools.partial(attend_back_kernel, block),
        [loc, pos, q, grad, attended, lse, kv, cos, sin, before],
        [shaped(*q.shape)] + [shaped(count // 2, rows, PAIR)] * 2,
        (),
        scores * 4600,
        scores,
        input_output_aliases={9: 0} if m else {},
        grid_spec=pltpu.PrefetchScalarGridSpec(
            num_scalar_prefetch=2,
            grid=(pieces,),
            in_specs=[
                heads,
                heads,
                heads,
                pl.BlockSpec((1, 1, 1, stacked), lambda p, *_: (p, m, 0, 0)),
                pl.BlockSpec((count, 1, rows, PAIR), lambda p, *_: (0, m, 0, 0)),
                table,
                table,
                ANY,
            ],
            out_specs=[heads, half, half],
            scratch_shapes=[
                pltpu.VMEM((count, rows, HD), BF),
                pltpu.VMEM((count, rows, HD), BF),
                pltpu.VMEM((count, HD, rows), BF),
                pltpu.VMEM((HD, stacked), F32),
                pltpu.VMEM((count, rows, HD), F32),
                pltpu.VMEM((count, rows, HD), F32),
            ],
        ),
        light=True,
    )


def rope_tables(positions):
    inverse = 1.0 / 10000.0 ** (jnp.arange(0, HD, 2).astype(F32) / HD)
    angle = positions.astype(F32)[:, None] * inverse[None, :]
    cos, sin = jnp.cos(angle), jnp.sin(angle)
    cos_head = jnp.concatenate([cos, cos], axis=1)
    sin_head = jnp.concatenate([-sin, sin], axis=1)
    ones, zeros = jnp.ones_like(cos_head), jnp.zeros_like(sin_head)
    return (
        jnp.concatenate([cos_head, cos_head], axis=1),
        jnp.concatenate([sin_head, sin_head], axis=1),
        jnp.concatenate([cos_head, ones], axis=1),
        jnp.concatenate([sin_head, zeros], axis=1),
    )


def normalize(values, gain):
    scale = lax.rsqrt(jnp.mean(values * values, axis=-1, keepdims=True) + EPSILON)
    return scale, (values * scale * gain).astype(BF)


def normalize_back(values, scale, gain, grad):
    norm = values * scale
    scaled = grad * gain
    inner = scale * (scaled - norm * jnp.mean(scaled * norm, axis=-1, keepdims=True))
    return inner, jnp.sum(grad * norm, axis=0)


class Sizes:
    def __init__(self, tokens, w_query):
        self.micro, self.held, self.width = tokens.shape
        self.rows = self.held // 2
        self.count = lax.axis_size("wide")
        self.depth = self.width // self.count
        self.heads = w_query.shape[2] // 2
        self.qkv = self.heads + PAIR


def shards(
    tokens, out_grad, attn_gain, w_query, w_key, w_value, w_out, ffn_gain, w_gate, w_up, w_down
):
    s = Sizes(tokens, w_query)
    section = lax.axis_index("section")
    wide = lax.axis_index("wide")
    core = lax.axis_index("tp")
    count, rows = s.count, s.rows
    home = section == 0

    pos = jnp.stack(
        [
            jnp.where((core ^ (p // 2)) == 0, 2 * wide, 2 * count - 1 - 2 * wide) * s.held
            + (section ^ (p % 2)) * rows
            for p in range(4)
        ]
    ).astype(jnp.int32)
    order = jnp.arange(4 * count)
    half_block = order // 2
    odd = half_block % 2
    owner = jnp.where(odd == 0, half_block, 2 * count - 1 - half_block) // 2
    loc = ((owner ^ wide) * 4 + (odd ^ core) * 2 + ((order % 2) ^ section)).astype(jnp.int32)
    positions = (pos[:, None] + jnp.arange(rows)[None, :]).reshape(-1)
    tables = rope_tables(positions)
    place = (tables, loc, pos)

    def halves(array, axis):
        size = array.shape[axis] // 2
        own = lax.dynamic_slice_in_dim(array, section * size, size, axis)
        away = lax.dynamic_slice_in_dim(array, (1 - section) * size, size, axis)
        return own, away

    def pack_attn(parts):
        query, key, value, out = parts
        return jnp.concatenate([query, key, value, out.T], axis=1)

    def both_layers(own, away):
        other = partner(away, "section", 1)
        return jnp.where(home, own, other), jnp.where(home, other, own)

    def take(values):
        part = lax.dynamic_slice_in_dim(values, section * rows, rows, 1)
        return mirror(part).reshape(-1, s.width)

    own_gains = jnp.concatenate([attn_gain, ffn_gain], axis=0)
    own_gains = lax.all_gather(own_gains, "wide", axis=1, tiled=True)
    gains_l = [gains.astype(F32) for gains in both_layers(own_gains, own_gains)]
    attn = [halves(w_query[0], 1), halves(w_key[0], 1), halves(w_value[0], 1), halves(w_out[0], 0)]
    attn_l = both_layers(*[pack_attn([part[i] for part in attn]) for i in range(2)])
    gate_h = halves(w_gate[0], 1)
    gate_l = both_layers(gate_h[0], after(gate_h[1], attn_l[0]))
    u = take(tokens).astype(F32)
    first_scale, low = normalize(u, gains_l[0][0])
    normed = spread(low)
    up_h, down_h = halves(w_up[0], 1), halves(w_down[0], 0)
    up_l = both_layers(up_h[0], after(up_h[1], normed[1]))
    down_l = both_layers(down_h[0].T, after(down_h[1].T, up_l[0]))

    gather_all = lambda x: lax.all_gather(x, "wide", axis=0, tiled=True)
    near = lambda x, *events: partner(after(x, *events), "wide", 1)
    attn_0 = gather_all(attn_l[0])
    gate_0 = gather_line(gate_l[0])
    up_0 = gather_line(up_l[0])
    q0, kv_own = qkv_project(normed, attn_0, tables, s.micro, s.qkv)
    down_0 = gather_line(after(down_l[0], q0))
    kv0 = jnp.concatenate(gather_blocks(kv_own), axis=0)
    attn_1 = gather_all(after(attn_l[1], q0))
    kv0, gate_0 = lax.optimization_barrier((kv0, gate_0))
    attended0, lse0 = attend(q0, kv0, loc, pos)
    gate_0 = (gate_0, near(gate_0))
    gate_1 = gather_line(after(gate_l[1], kv0))
    own, send = contract(
        [after(attended0, gate_0[1]).reshape(-1, s.heads)],
        [(attn_0,)],
        (s.qkv,),
        s.depth,
        s.width,
    )
    up_0 = (up_0, near(up_0, gate_0[1], own))
    upstream = take(after(out_grad, own))
    normed_ffn0, middle0, second_scale0, _ = exchange(
        own, send, u, gains_l[0][1], ident=0
    )
    up_1 = gather_line(after(up_l[1], middle0))
    line_down0 = down_0
    down_0 = (down_0, near(down_0, up_0[1], middle0))
    gate0, up0, hidden0 = gate_up(
        [after(normed_ffn0[0], up_0[1], upstream, line_down0), *normed_ffn0[1:]],
        gate_0,
        up_0,
        s.depth,
    )
    upstream_other = after(partner(after(upstream, up_0[1]), "section", 1), hidden0)
    down_1 = gather_line(after(down_l[1], hidden0))
    gate_1 = (gate_1, near(gate_1, down_0[1]))
    own, send = contract(
        [after(hidden0, upstream_other)], [down_0], (None,), s.depth, s.width
    )
    kept0 = (u, first_scale, normed, q0, kv0, attended0, lse0, middle0, second_scale0)
    kept0 += (normed_ffn0, gate0, up0, hidden0)
    normed, u, first_scale, _ = exchange(
        own, send, middle0, gains_l[1][0], keep_f32=False, ident=1
    )
    out0 = u
    q1, kv_own = qkv_project(
        [after(normed[0], gate_1[1]), *normed[1:]], attn_1, tables, s.micro, s.qkv
    )
    kv1 = jnp.concatenate(gather_blocks(kv_own), axis=0)
    up_1 = (up_1, near(up_1, kv1))
    attended1, lse1 = attend(q1, after(kv1, up_1[0]), loc, pos)
    own, send = contract(
        [after(attended1, up_1[1], down_1).reshape(-1, s.heads)], [(attn_1,)], (s.qkv,), s.depth, s.width
    )
    down_1 = (down_1, near(down_1, up_1[1], own))
    normed_ffn1, middle1, second_scale1, _ = exchange(own, send, u, gains_l[1][1], ident=5)
    grad2 = [upstream, upstream_other]
    grad2 += [partner(after(x, normed_ffn1[0]), "tp", 1) for x in grad2]
    gate1, up1, hidden1 = gate_up(
        [after(normed_ffn1[0], down_1[1]), *normed_ffn1[1:]], gate_1, up_1, s.depth
    )
    kept1 = (u, first_scale, normed, q1, kv1, attended1, lse1, middle1, second_scale1)
    kept1 += (normed_ffn1, gate1, up1, hidden1)
    own1, send1 = contract([hidden1], [down_1], (None,), s.depth, s.width)
    layers = [
        (gains_l[0], attn_0, gate_0, up_0, down_0),
        (gains_l[1], attn_1, gate_1, up_1, down_1),
    ]
    kept = [kept0, kept1]

    def near_sum(keep, got):
        total = (keep.astype(F32) + got.astype(F32)).astype(BF)
        return total.reshape(-1, total.shape[-1])

    reduce_all = lambda x: lax.psum_scatter(x, "wide", scatter_dimension=0, tiled=True)

    def give(value, layer):
        value = value.reshape(s.micro, rows, s.width)
        pair = [mirror(value, 0, (layer,)), mirror(value, 1, (1 - layer,))]
        return jnp.concatenate(pair[::-1] if layer else pair, axis=1)

    grads, terms, gain_terms = [None, None], [None, None], []
    by_piece = lambda table: table.reshape(4, rows, PAIR)
    halved = lambda x: x.reshape(count // 2, 4, rows, PAIR)
    for layer in (1, 0):
        gains, attn, gate_w, up_w, down_w = layers[layer]
        u, first_scale, normed, q, kv, attended, lse, middle, second_scale, normed_ffn = kept[
            layer
        ][:10]
        gate, up, hidden = kept[layer][10:]
        flat = attended.reshape(-1, s.heads)
        if layer:
            grad2 = [after(x, own1) for x in grad2]
            given0 = give(after(out0, own1), 0)
        down_send, down_keep = weight_grad(grad2, [hidden], count)
        down_got = partner(down_send, "wide", 1)
        grad_gate, grad_up = hidden_back(
            [after(x, down_send) for x in grad2], down_w, gate, up, s.depth
        )
        gate_send, gate_keep = weight_grad(normed_ffn, [grad_gate], count)
        up_send, up_keep = weight_grad(
            [after(x, gate_send) for x in normed_ffn], [grad_up], count
        )
        if layer:
            out1 = (middle1 + fold(own1, send1)).astype(BF)
            grad_gate, given0 = lax.optimization_barrier((after(grad_gate, out1), given0))
        own, send = contract(
            [after(grad_gate, up_send), grad_up],
            [gate_w, up_w],
            (None, None),
            s.depth,
            s.width,
        )
        down_near = near_sum(down_keep, after(down_got, own))
        if layer == 0:
            own = after(own, d_attn)
            terms[1][0] = d_attn
        d_down = reduce_line(down_near)
        gate_got = partner(after(gate_send, down_near), "wide", 1)
        grad1, grad_middle, second_gain, _ = exchange(
            after(own, down_near), send, upstream, gains[1], middle, second_scale, ident=2
        )
        gate_got, d_down = after((gate_got, d_down), grad1[0])
        gate_near = near_sum(gate_keep, gate_got)
        d_gate = reduce_line(gate_near)
        up_got = partner(after(up_send, gate_near, d_down), "wide", 1)
        grad1 = [after(grad1[0], gate_near, d_down), *grad1[1:]]
        grad_attended = out_back(grad1, attn, s.qkv, s.heads)
        if layer == 0:
            crossed = [partner_one(x, 0) for x in after(tuple(terms[1]), grad_attended)]
        else:
            given1 = give(after(out1, grad_attended), 1)
        back = lambda m, grad, before: attend_back(
            m, q, grad, attended, lse, kv, tables[0], tables[1], loc, pos, before
        )
        grad_attended = grad_attended.reshape(q.shape)
        dq, send0, keep0 = back(0, grad_attended, q)
        got0 = partner(halved(send0), "wide", 1)
        if layer == 0:
            down_crossed = partner_one(after(d_down, send0), 1)
        dq, send1_, keep1 = back(1, after(grad_attended, send0), dq)
        if layer == 0:
            dq, down_crossed = lax.optimization_barrier((dq, down_crossed))
        up_got, got0, d_gate = after((up_got, got0, d_gate), dq)
        near0 = reduce_near(halved(keep0), got0)
        if layer == 0:
            gate_crossed = partner_one(after(d_gate, near0), 1)
        got1 = partner(after(halved(send1_), near0), "wide", 1)
        dkv0 = reduce_far(near0)
        up_near = near_sum(up_keep, after(up_got, near0))
        d_up = reduce_line(up_near)
        out_send, out_keep = weight_grad(
            [after(x, up_near, d_gate) for x in grad1], [flat], count
        )
        if layer:
            out_send, given1 = lax.optimization_barrier((out_send, given1))
            section_out = jnp.where(home, given0, given1)
        dkv1 = reduce_far(reduce_near(halved(keep1), after(got1, out_send)))
        if layer == 0:
            crossed = list(after(tuple(crossed), dq))
            dkv1 = after(dkv1, *crossed)
        half = HD // 2
        back_rows = []
        for dkv in (dkv0, dkv1):
            turned = jnp.concatenate(
                [dkv[..., half:HD], dkv[..., :half], jnp.zeros_like(dkv[..., HD:])], axis=-1
            )
            back_rows.append(dkv * by_piece(tables[2]) - turned * by_piece(tables[3]))
        dkv = jnp.stack(back_rows, axis=1).astype(BF)
        dq, dkv = after(dq, out_send).reshape(-1, s.heads), dkv.reshape(-1, PAIR)
        if layer == 0:
            out_got = partner(after(out_send, got1), "wide", 1)
            dkv, gate_crossed = lax.optimization_barrier((dkv, gate_crossed))
            crossed_0 = [gate_crossed, down_crossed]
        own, send = contract([dq, dkv], [(attn,), (attn,)], (0, s.heads), s.depth, s.width)
        if layer == 0:
            out_near = near_sum(out_keep, after(out_got, own))
            d_out = reduce_line(out_near)
            own = after(own, out_near)
        qkv_send, qkv_keep = weight_grad(
            [after(x, own) for x in normed], [dq, dkv], count
        )
        if layer:
            pack_got = partner(
                jnp.concatenate([after(qkv_send, dkv1), out_send], axis=2), "wide", 1
            )
            grad2, _, first_gain, _ = exchange(
                after(own, qkv_send),
                send,
                grad_middle,
                gains[0],
                u,
                first_scale,
                keep_f32=False,
                ident=3,
            )
            grads[1] = upstream = grad2[0]
            pack_got, d_up = after((pack_got, d_up), grad2[0])
            pack_near = near_sum(jnp.concatenate([qkv_keep, out_keep], axis=2), pack_got)
            d_attn = reduce_line(after(pack_near, d_up))
            grad2 = [after(x, pack_near) for x in grad2]
            terms[1] = [None, d_gate, d_up, d_down]
        else:
            grads[0], _, first_gain, got = exchange(
                own,
                send,
                grad_middle,
                gains[0],
                u,
                first_scale,
                keep_f32=False,
                last=True,
                bulk=(qkv_send,),
                ident=4,
            )
            grads[0] = grads[0][0]
            qkv_near = near_sum(qkv_keep, got[0])
            grads_out = give(after(grads[1], grads[0]), 1)
            blocks = qkv_near.reshape(count // 2, s.depth, -1)
            d_qkv = blocks[wide // 2].astype(F32)
            for j in range(1, count // 2):
                block = partner(blocks[(wide // 2) ^ j], "wide", 2 * j)
                d_qkv = d_qkv + block.astype(F32)
            d_qkv = d_qkv.astype(BF)
            terms[0] = [d_qkv, d_out, d_gate, d_up, d_down]
        gain_terms += [first_gain.reshape(1, -1), second_gain.reshape(1, -1)]

    given = (give(grads[0], 0), grads_out)
    up_crossed = partner_one(after(d_up, grads[0]), 1)
    d_qkv_out, *given = lax.optimization_barrier((d_qkv, *given))
    input_grads = jnp.where(home, *given)
    late = [partner_one(x, 1) for x in (d_qkv_out, d_out)]
    crossed_0 = [*late, crossed_0[0], up_crossed, crossed_0[1]]
    crossed = [crossed[0][:, : s.qkv], crossed[0][:, s.qkv :], *crossed[1:]]
    terms[1] = [terms[1][0][:, : s.qkv], terms[1][0][:, s.qkv :], *terms[1][1:]]
    gain_total = jnp.concatenate(gain_terms, axis=0)
    gain_total = gain_total + partner(gain_total, "tp", 1)
    gain_total = gain_total + partner(gain_total, "section", 1)
    gain_total = gain_total.reshape(4, count // 2, 2, s.depth)
    gain_total = gain_total[:, :, side()] + partner(gain_total[:, :, 1 - side()], "wide", 1)
    total = gain_total[:, wide // 2]
    for j in range(1, count // 2):
        total = total + partner(gain_total[:, (wide // 2) ^ j], "wide", 2 * j)
    gain_total = total
    gains = jnp.where(home, gain_total[2:], gain_total[:2])

    def settle(index):
        own = jnp.where(home, terms[0][index], terms[1][index]).astype(F32)
        other = crossed[index].astype(F32) + crossed_0[index].astype(F32)
        return jnp.where(home, own, other), jnp.where(home, other, own)

    heads = s.heads
    low, high = settle(0)
    cut = lambda start, size: jnp.concatenate(
        [low[:, start : start + size], high[:, start : start + size]], axis=1
    )
    d_query = cut(0, heads)
    d_key = cut(heads, HD)
    d_value = cut(heads + HD, HD)
    d_out = jnp.concatenate([half.T for half in settle(1)], axis=0)
    d_gate = jnp.concatenate(settle(2), axis=1)
    d_up = jnp.concatenate(settle(3), axis=1)
    d_down = jnp.concatenate([half.T for half in settle(4)], axis=0)
    return (
        section_out[None],
        input_grads[None],
        gains[0:1],
        d_query[None],
        d_key[None],
        d_value[None],
        d_out[None],
        gains[1:2],
        d_gate[None],
        d_up[None],
        d_down[None],
    )


def solution(mesh):
    return jax.shard_map(
        shards,
        mesh=mesh,
        in_specs=(
            P(None, ("wide", "tp"), None),
            P(None, ("wide", "tp"), None),
            P("section", "wide"),
            P("section", "wide", "tp"),
            P("section", "wide", "tp"),
            P("section", "wide", "tp"),
            P("section", "tp", "wide"),
            P("section", "wide"),
            P("section", "wide", "tp"),
            P("section", "wide", "tp"),
            P("section", "tp", "wide"),
        ),
        out_specs=(
            P("section", None, ("wide", "tp"), None),
            P("section", None, ("wide", "tp"), None),
            P("section", "wide"),
            P("section", "wide", "tp"),
            P("section", "wide", "tp"),
            P("section", "wide", "tp"),
            P("section", "tp", "wide"),
            P("section", "wide"),
            P("section", "wide", "tp"),
            P("section", "wide", "tp"),
            P("section", "tp", "wide"),
        ),
        check_vma=False,
    )
```

```python
import functools
import math

import jax
import jax.numpy as jnp
from jax import lax
from jax.experimental import pallas as pl
from jax.experimental.pallas import tpu as pltpu
from jax.sharding import PartitionSpec as P

HD = 64
PAIR = 2 * HD
EPSILON = 1e-05
GAIN_ROWS = 16
VMEM = 48 * 2**20
BF = jnp.bfloat16
F32 = jnp.float32
ANY = pl.BlockSpec(memory_space=pl.ANY)


def partner(x, axis, bit):
    peers = lax.axis_size(axis)
    return lax.ppermute(x, axis, [(i, i ^ bit) for i in range(peers)])


def partner_one(x, source):
    return lax.ppermute(x, "section", [(source, 1 - source)])


def after(value, *events):
    return lax.optimization_barrier((value,) + events)[0]


def product(left, right):
    return jnp.dot(left, right, preferred_element_type=F32)


def cross(left, right):
    return lax.dot_general(left, right, (((0,), (0,)), ((), ())), preferred_element_type=F32)


def against(left, right):
    return lax.dot_general(left, right, (((1,), (1,)), ((), ())), preferred_element_type=F32)


def call(body, ins, outs, scratch, flops, exps=0, ident=None, light=False, **more):
    moved = sum(x.size * x.dtype.itemsize for x in list(ins) + list(outs))
    if light:
        moved, flops, exps = moved // 8, flops // 8, exps // 8
    remote = {} if ident is None else {"collective_id": ident, "has_side_effects": True}
    return pl.pallas_call(
        body,
        out_shape=outs,
        scratch_shapes=scratch,
        compiler_params=pltpu.CompilerParams(vmem_limit_bytes=VMEM, **remote),
        cost_estimate=pl.CostEstimate(
            flops=int(flops), bytes_accessed=int(moved), transcendentals=int(exps)
        ),
        **more,
    )(*ins)


def shaped(*dims, kind=BF):
    return jax.ShapeDtypeStruct(dims, kind)


def lines():
    count = lax.axis_size("wide")
    return [list(range(y, count, 2)) for y in range(2)]


def side():
    return lax.axis_index("wide") % 2


def gather_line(shard):
    return lax.all_gather(shard, "wide", axis=0, tiled=True, axis_index_groups=lines())


def reduce_line(near):
    return lax.psum_scatter(
        near, "wide", scatter_dimension=0, tiled=True, axis_index_groups=lines()
    )


def gather_blocks(shard):
    count = lax.axis_size("wide")
    far = [shard if k == 0 else partner(shard, "wide", k) for k in range(0, count, 2)]
    blocks = []
    for block in far:
        blocks += [block, partner(block, "wide", 1)]
    return blocks


def reduce_near(keep, got):
    return keep.astype(F32) + got.astype(F32)


def reduce_far(near):
    total = near[0]
    for j in range(1, near.shape[0]):
        total = total + partner(near[j].astype(BF), "wide", 2 * j).astype(F32)
    return total


def mirror(x, cross=0, sections=(0, 1)):
    count = lax.axis_size("wide")
    pairs = []
    for section in sections:
        for w in range(count):
            for core in range(2):
                to = w if core == 0 else count - 1 - w
                pairs.append(
                    ((section * count + w) * 2 + core, ((section ^ cross) * count + to) * 2 + core)
                )
    return lax.ppermute(x, ("section", "wide", "tp"), pairs)


def spread(values):
    other = partner(values, "section", 1)
    return [values, other, partner(values, "tp", 1), partner(other, "tp", 1)]


def fold(own, send):
    rows = own.shape[0] // 2
    got = partner(send, "tp", 1)
    away = (own[rows:].astype(F32) + got[rows:].astype(F32)).astype(BF)
    mine = own[:rows].astype(F32) + got[:rows].astype(F32)
    return mine + partner(away, "section", 1).astype(F32)


def load_attn(ref, dest, sem, start):
    copy = pltpu.make_async_copy(ref.at[:, pl.ds(start, dest.shape[1])], dest, sem.at[0])
    copy.start()
    return [copy]


def load_sides(refs, dest, sem, depth, first=0):
    copies = []
    if len(refs) == 1:
        copies.append(pltpu.make_async_copy(refs[0], dest, sem.at[first]))
        copies[-1].start()
        return copies
    y = side()
    for s, ref in enumerate(refs):
        for j in range(dest.shape[0] // (2 * depth)):
            place = pl.multiple_of((2 * j + (y + s) % 2) * depth, depth)
            copies.append(
                pltpu.make_async_copy(
                    ref.at[pl.ds(j * depth, depth)],
                    dest.at[pl.ds(place, depth)],
                    sem.at[first + 2 * j + s],
                )
            )
            copies[-1].start()
    return copies


def exchange_kernel(back, keep_f32, last, bulk, *refs):
    own_ref, send_ref, base_ref, gain_ref = refs[:4]
    refs = refs[4:]
    if back:
        values_ref, scale_ref = refs[:2]
        refs = refs[2:]
    bulk_in, refs = refs[:bulk], refs[bulk:]
    held = 1 if last else 4
    pieces, refs = refs[:held], refs[held:]
    first_out, second_out = refs[:2]
    bulk_out, refs = refs[2 : 2 + bulk], refs[2 + bulk :]
    got_tp, away, got_section, low, send_sem, recv_sem, local_sem, bulk_sem = refs
    rows, width = low.shape
    chunks = 4
    size = rows // chunks
    peers = {
        "tp": {"tp": 1 - lax.axis_index("tp")},
        "section": {"section": 1 - lax.axis_index("section")},
        "near": {"wide": lax.axis_index("wide") + 1 - 2 * side()},
    }
    greeted = ["tp", "section"] + (["near"] if bulk else [])
    barrier = pltpu.get_barrier_semaphore()
    for name in greeted:
        pl.semaphore_signal(
            barrier, inc=1, device_id=peers[name], device_id_type=pl.DeviceIdType.MESH
        )
    pl.semaphore_wait(barrier, len(greeted))

    def remote(source, target, index, name):
        copy = pltpu.make_async_remote_copy(
            src_ref=source,
            dst_ref=target,
            send_sem=send_sem.at[index],
            recv_sem=recv_sem.at[index],
            device_id=peers[name],
            device_id_type=pl.DeviceIdType.MESH,
        )
        copy.start()
        return copy

    bulk_copies = [
        pltpu.make_async_remote_copy(
            src_ref=bulk_in[i],
            dst_ref=bulk_out[i],
            send_sem=bulk_sem.at[0, i],
            recv_sem=bulk_sem.at[1, i],
            device_id=peers["near"],
            device_id_type=pl.DeviceIdType.MESH,
        )
        for i in range(bulk)
    ]
    for copy in bulk_copies:
        copy.start()
    span = lambda c: pl.ds(c * size, size)
    sums = [
        remote(send_ref.at[pl.ds(rows, rows)], got_tp.at[1], 0, "tp"),
        remote(send_ref.at[pl.ds(0, rows)], got_tp.at[0], 1, "tp"),
    ]
    sums[0].wait()
    crossing = []
    for c in range(chunks):
        total = own_ref[rows + c * size : rows + (c + 1) * size].astype(F32)
        away[span(c)] = (total + got_tp[1, span(c)].astype(F32)).astype(BF)
        crossing.append(remote(away.at[span(c)], got_section.at[span(c)], 2 + c, "section"))
    sums[1].wait()
    over_section, over_tp, local = [], [], []
    gain = gain_ref[...]
    gain_total = jnp.zeros((1, width), F32)
    for c in range(chunks):
        here = slice(c * size, (c + 1) * size)
        crossing[c].wait()
        total = own_ref[here].astype(F32) + got_tp[0, here].astype(F32)
        total = total + got_section[here].astype(F32)
        base = base_ref[here].astype(F32)
        if back:
            scale = scale_ref[here]
            norm = values_ref[here].astype(F32) * scale
            scaled = total * gain
            mean = jnp.mean(scaled * norm, axis=-1, keepdims=True)
            gain_total = gain_total + jnp.sum(total * norm, axis=0, keepdims=True)
            result = base + scale * (scaled - norm * mean)
            if keep_f32:
                first_out[here] = result
            low[here] = result.astype(BF)
        else:
            result = base + total
            if keep_f32:
                first_out[here] = result
            else:
                first_out[here] = result.astype(BF)
                result = result.astype(BF).astype(F32)
            scale = lax.rsqrt(jnp.mean(result * result, axis=-1, keepdims=True) + EPSILON)
            second_out[here] = scale
            low[here] = (result * scale * gain).astype(BF)
        copy = pltpu.make_async_copy(low.at[span(c)], pieces[0].at[span(c)], local_sem.at[c])
        copy.start()
        local.append(copy)
        if last:
            continue
        over_section.append(
            remote(low.at[span(c)], pieces[1].at[span(c)], 2 + chunks + c, "section")
        )
        over_tp.append(remote(low.at[span(c)], pieces[2].at[span(c)], 2 + 2 * chunks + c, "tp"))
    if back:
        second_out[...] = gain_total
        if not keep_f32:
            first_out[...] = gain_total
    forwarded = []
    for c in range(0 if last else chunks):
        over_section[c].wait()
        forwarded.append(
            remote(pieces[1].at[span(c)], pieces[3].at[span(c)], 2 + 3 * chunks + c, "tp")
        )
    for copy in local + over_tp + forwarded + bulk_copies:
        copy.wait()


def exchange(
    own, send, base, gain, values=None, scale=None, keep_f32=True, last=False, bulk=(), ident=0
):
    rows, width = base.shape
    back = values is not None
    vmem = pl.BlockSpec(memory_space=pltpu.VMEM)
    ins = [own, send, base, gain.reshape(1, width)] + ([values, scale] if back else [])
    piece = shaped(rows, width)
    if back:
        first = shaped(rows, width, kind=F32) if keep_f32 else shaped(1, width, kind=F32)
        second = shaped(1, width, kind=F32)
    else:
        first = shaped(rows, width, kind=F32 if keep_f32 else BF)
        second = shaped(rows, 1, kind=F32)
    count = 2 + 4 * 4
    held = 1 if last else 4
    outs = call(
        functools.partial(exchange_kernel, back, keep_f32, last, len(bulk)),
        [*ins, *bulk],
        [piece] * held + [first, second] + [shaped(*x.shape) for x in bulk],
        [
            pltpu.VMEM((2, rows, width), BF),
            pltpu.VMEM((rows, width), BF),
            pltpu.VMEM((rows, width), BF),
            pltpu.VMEM((rows, width), BF),
            pltpu.SemaphoreType.DMA((count,)),
            pltpu.SemaphoreType.DMA((count,)),
            pltpu.SemaphoreType.DMA((4,)),
            pltpu.SemaphoreType.DMA((2, max(1, len(bulk)))),
        ],
        60e9,
        ident=ident,
        light=back,
        in_specs=[vmem] * len(ins) + [ANY] * len(bulk),
        out_specs=[ANY] * held + [vmem] * 2 + [ANY] * len(bulk),
    )
    return outs[:held], outs[held], outs[held + 1], outs[held + 2 :]


def qkv_kernel(*refs):
    pieces, attn, tables = refs[:4], refs[4], refs[5:9]
    q_ref, kv_ref, w, sem = refs[9:]
    width = w.shape[1]
    for copy in load_attn(attn, w, sem, 0):
        copy.wait()
    cos, sin, cos_kv, sin_kv = tables
    for p, piece in enumerate(pieces):
        linear = product(piece[...], w[...])
        micro, rows = q_ref.shape[1], q_ref.shape[2]
        first = lax.broadcasted_iota(jnp.int32, (rows, PAIR), 1) % HD < HD // 2
        span = slice(p * rows, (p + 1) * rows)
        for m in range(micro):
            for start in range(0, width, PAIR):
                part = linear[m * rows : (m + 1) * rows, start : start + PAIR]
                turned = jnp.where(
                    first, pltpu.roll(part, PAIR - HD // 2, 1), pltpu.roll(part, HD // 2, 1)
                )
                if start + PAIR < width:
                    out = part * cos[span] + turned * sin[span]
                    q_ref[p, m, :, start : start + PAIR] = out.astype(BF)
                else:
                    out = part * cos_kv[span] + turned * sin_kv[span]
                    kv_ref[p, m] = out.astype(BF)


def qkv_project(pieces, attn, tables, micro, width):
    total, d = pieces[0].shape
    rows = total // micro
    vmem = pl.BlockSpec(memory_space=pltpu.VMEM)
    return call(
        qkv_kernel,
        [*pieces, attn, *tables],
        [shaped(4, micro, rows, width - PAIR), shaped(4, micro, rows, PAIR)],
        [pltpu.VMEM((d, width), BF), pltpu.SemaphoreType.DMA((1,))],
        8 * total * d * width,
        in_specs=[vmem] * 4 + [ANY] + [vmem] * 4,
        out_specs=[vmem] * 2,
    )


def gate_up_kernel(depth, sides, *refs):
    pieces, refs = refs[:4], refs[4:]
    gates, ups, refs = refs[: sides[0]], refs[sides[0] : sum(sides)], refs[sum(sides) :]
    outs = refs[:3]
    x, w_gate, w_up, buffer, x_sem, w_sem, out_sem = refs[3:]
    copies = load_sides(gates, w_gate, w_sem, depth)
    copies += load_sides(ups, w_up, w_sem, depth, w_gate.shape[0] // depth)
    inputs = []
    for p, piece in enumerate(pieces):
        inputs.append(pltpu.make_async_copy(piece, x.at[p], x_sem.at[p]))
        inputs[-1].start()
    for copy in copies:
        copy.wait()
    rows = x.shape[1]
    results = []
    for p in range(4):
        inputs[p].wait()
        gate = product(x[p], w_gate[...])
        up = product(x[p], w_up[...])
        if p >= 2:
            for copy in results[p - 2]:
                copy.wait()
        slot = p % 2
        buffer[slot, 0] = gate.astype(BF)
        buffer[slot, 1] = up.astype(BF)
        buffer[slot, 2] = (gate * jax.nn.sigmoid(gate) * up).astype(BF)
        results.append(
            [
                pltpu.make_async_copy(
                    buffer.at[slot, i], outs[i].at[pl.ds(p * rows, rows)], out_sem.at[p, i]
                )
                for i in range(3)
            ]
        )
        for copy in results[p]:
            copy.start()
    for p in (2, 3):
        for copy in results[p]:
            copy.wait()


def gate_up(pieces, gates, ups, depth):
    rows, d = pieces[0].shape
    hidden = gates[0].shape[1]
    return call(
        functools.partial(gate_up_kernel, depth, (len(gates), len(ups))),
        [*pieces, *gates, *ups],
        [shaped(4 * rows, hidden)] * 3,
        [
            pltpu.VMEM((4, rows, d), BF),
            pltpu.VMEM((d, hidden), BF),
            pltpu.VMEM((d, hidden), BF),
            pltpu.VMEM((2, 3, rows, hidden), BF),
            pltpu.SemaphoreType.DMA((4,)),
            pltpu.SemaphoreType.DMA((2 * d // depth,)),
            pltpu.SemaphoreType.DMA((4, 3)),
        ],
        16 * rows * d * hidden,
        4 * rows * hidden,
        in_specs=[ANY] * (4 + len(gates) + len(ups)),
        out_specs=[ANY] * 3,
    )


def hidden_back_kernel(depth, *refs):
    pieces, downs = refs[:4], refs[4:6]
    gate_ref, up_ref = refs[6:8]
    outs = refs[8:10]
    x, w, kept, buffer, x_sem, w_sem, kept_sem, out_sem = refs[10:]
    copies = load_sides(downs, w, w_sem, depth)
    rows = x.shape[1]
    inputs = []
    for p, piece in enumerate(pieces):
        span = pl.ds(p * rows, rows)
        inputs.append(
            [
                pltpu.make_async_copy(piece, x.at[p], x_sem.at[p]),
                pltpu.make_async_copy(gate_ref.at[span], kept.at[p, 0], kept_sem.at[p, 0]),
                pltpu.make_async_copy(up_ref.at[span], kept.at[p, 1], kept_sem.at[p, 1]),
            ]
        )
        for copy in inputs[-1]:
            copy.start()
    for copy in copies:
        copy.wait()
    results = []
    for p in range(4):
        for copy in inputs[p]:
            copy.wait()
        grad = product(x[p], w[...])
        gate = kept[p, 0].astype(F32)
        up = kept[p, 1].astype(F32)
        sigma = jax.nn.sigmoid(gate)
        if p >= 2:
            for copy in results[p - 2]:
                copy.wait()
        slot = p % 2
        buffer[slot, 0] = (grad * up * sigma * (1.0 + gate * (1.0 - sigma))).astype(BF)
        buffer[slot, 1] = (grad * gate * sigma).astype(BF)
        results.append(
            [
                pltpu.make_async_copy(
                    buffer.at[slot, i], outs[i].at[pl.ds(p * rows, rows)], out_sem.at[p, i]
                )
                for i in range(2)
            ]
        )
        for copy in results[p]:
            copy.start()
    for p in (2, 3):
        for copy in results[p]:
            copy.wait()


def hidden_back(pieces, downs, gate, up, depth):
    rows, d = pieces[0].shape
    hidden = downs[0].shape[1]
    return call(
        functools.partial(hidden_back_kernel, depth),
        [*pieces, *downs, gate, up],
        [shaped(4 * rows, hidden)] * 2,
        [
            pltpu.VMEM((4, rows, d), BF),
            pltpu.VMEM((d, hidden), BF),
            pltpu.VMEM((4, 2, rows, hidden), BF),
            pltpu.VMEM((2, 2, rows, hidden), BF),
            pltpu.SemaphoreType.DMA((4,)),
            pltpu.SemaphoreType.DMA((d // depth,)),
            pltpu.SemaphoreType.DMA((4, 2)),
            pltpu.SemaphoreType.DMA((4, 2)),
        ],
        8 * rows * d * hidden,
        4 * rows * hidden,
        in_specs=[ANY] * 8,
        out_specs=[ANY] * 2,
        light=True,
    )


def out_back_kernel(offset, *refs):
    pieces, attn = refs[:4], refs[4]
    out_ref, w, sem = refs[5:]
    for copy in load_attn(attn, w, sem, offset):
        copy.wait()
    rows = pieces[0].shape[0]
    for p, piece in enumerate(pieces):
        out_ref[p * rows : (p + 1) * rows] = product(piece[...], w[...]).astype(BF)


def out_back(pieces, attn, offset, width):
    rows, d = pieces[0].shape
    vmem = pl.BlockSpec(memory_space=pltpu.VMEM)
    return call(
        functools.partial(out_back_kernel, offset),
        [*pieces, attn],
        [shaped(4 * rows, width)],
        [pltpu.VMEM((d, width), BF), pltpu.SemaphoreType.DMA((1,))],
        8 * rows * d * width,
        in_specs=[vmem] * 4 + [ANY],
        out_specs=[vmem],
        light=True,
    )[0]


def contract_kernel(depth, starts, sizes, *refs):
    sides = len(starts)
    lefts, refs = refs[:sides], refs[sides:]
    sources = []
    for size in sizes:
        sources.append(refs[:size])
        refs = refs[size:]
    own_ref, send_ref = refs[:2]
    weights, sem = refs[2:-1], refs[-1]
    step = pl.program_id(0)
    half = pl.num_programs(0) // 2

    @pl.when(step == 0)
    def _():
        copies = []
        for s, start in enumerate(starts):
            if start is None:
                copies += load_sides(sources[s], weights[s], sem.at[s], depth)
            else:
                copies += load_attn(sources[s][0], weights[s], sem.at[s], start)
        for copy in copies:
            copy.wait()

    total = against(lefts[0][...], weights[0][...])
    for s in range(1, sides):
        total = total + against(lefts[s][...], weights[s][...])
    total = total.astype(BF)

    @pl.when(step < half)
    def _():
        send_ref[...] = total

    @pl.when(step >= half)
    def _():
        own_ref[...] = total


def contract(lefts, sources, starts, depth, width):
    sides = len(lefts)
    total = lefts[0].shape[0]
    tile = total // 4
    flat = [ref for group in sources for ref in group]
    return call(
        functools.partial(contract_kernel, depth, starts, [len(group) for group in sources]),
        [*lefts, *flat],
        [shaped(total // 2, width)] * 2,
        [pltpu.VMEM((width, left.shape[1]), BF) for left in lefts]
        + [pltpu.SemaphoreType.DMA((sides, width // depth))],
        sum(2 * total * left.shape[1] * width for left in lefts),
        grid=(4,),
        in_specs=[
            pl.BlockSpec((tile, left.shape[1]), lambda i: ((i + 2) % 4, 0)) for left in lefts
        ]
        + [ANY] * len(flat),
        out_specs=[
            pl.BlockSpec((tile, width), lambda i: (jnp.maximum(i - 2, 0), 0)),
            pl.BlockSpec((tile, width), lambda i: (jnp.minimum(i, 1), 0)),
        ],
    )


def weight_kernel(rights, split, *refs):
    pieces, right_refs, outs = refs[:4], refs[4 : 4 + rights], refs[4 + rights :]
    left = jnp.concatenate([x[...] for x in pieces], axis=0)
    start = 0
    for right in right_refs:
        grad = cross(left, right[...]).astype(BF)
        span = slice(start, start + right.shape[1])
        start += right.shape[1]
        if not split:
            outs[0][:, span] = grad
            continue
        send_ref, keep_ref = outs
        depth = keep_ref.shape[1]
        for y, (first, second) in enumerate(((keep_ref, send_ref), (send_ref, keep_ref))):

            @pl.when(side() == y)
            def _():
                first[0, :, span] = grad[:depth]
                second[0, :, span] = grad[depth:]


def weight_grad(pieces, rights, n, split=True):
    rows, d = pieces[0].shape
    width = sum(right.shape[1] for right in rights)
    depth = d // n
    if split:
        shapes = [shaped(n // 2, depth, width)] * 2
        specs = [pl.BlockSpec((1, depth, width), lambda j: (j, 0, 0))] * 2
    else:
        shapes = [shaped(d, width)]
        specs = [pl.BlockSpec((2 * depth, width), lambda j: (j, 0))]
    outs = call(
        functools.partial(weight_kernel, len(rights), split),
        [*pieces, *rights],
        shapes,
        [],
        8 * rows * d * width,
        grid=(n // 2,),
        in_specs=[pl.BlockSpec((rows, 2 * depth), lambda j: (0, j))] * 4
        + [pl.BlockSpec(right.shape, lambda j: (0, 0)) for right in rights],
        out_specs=specs,
        light=True,
    )
    return outs if split else outs[0]


def stack_heads(x):
    return jnp.concatenate([x[:, h : h + HD] for h in range(0, x.shape[1], HD)], axis=0)


def turn_heads(x):
    pairs = [x[:, g : g + PAIR].T for g in range(0, x.shape[1], PAIR)]
    return jnp.concatenate([part for pair in pairs for part in (pair[:HD], pair[HD:])], axis=1)


def back_heads(x, rows, g):
    even = x[:, 2 * g * rows : (2 * g + 1) * rows]
    odd = x[:, (2 * g + 1) * rows : (2 * g + 2) * rows]
    return jnp.concatenate([even, odd], axis=0).T


def attend_kernel(
    block, loc_ref, pos_ref, q_ref, kv_ref, o_ref, lse_ref, k_ref, vt_ref, m_ref, acc_ref, s_ref
):
    piece = pl.program_id(1)
    rows = q_ref.shape[2]
    count = kv_ref.shape[0]
    per_block = block // rows

    @pl.when(piece == 0)
    def _():
        def one(i, _):
            kv = kv_ref[loc_ref[i], 0]
            k_ref[i] = kv[:, :HD]
            ones = jnp.ones((GAIN_ROWS, rows), BF)
            vt_ref[i] = jnp.concatenate([kv.T[HD:], ones], axis=0)
            return 0

        lax.fori_loop(0, count, one, 0)

    pos = pos_ref[piece]
    queries = turn_heads(q_ref[0, 0] * BF(1.0 / math.sqrt(HD)))
    m_ref[...] = jnp.full(m_ref.shape, -1e30, F32)
    acc_ref[...] = jnp.zeros(acc_ref.shape, F32)

    def scores_of(j):
        first = j * per_block
        keys = jnp.concatenate([k_ref[first + i] for i in range(per_block)], axis=0)
        return product(keys, queries)

    def absorb(j, scores):
        first = j * per_block
        used = scores.shape[0] // rows
        values = jnp.concatenate([vt_ref[first + i] for i in range(used)], axis=1)
        before = m_ref[...]
        now = jnp.maximum(before, jnp.max(scores, axis=0, keepdims=True))
        terms = jnp.exp(scores - now)
        shrink = jnp.exp(before - now)
        acc_ref[...] = acc_ref[...] * shrink + product(values, terms.astype(BF))
        m_ref[...] = now

    full = pos // block
    s_ref[0] = scores_of(0)

    def loop(j, _):
        slot = j % 2
        following = scores_of(j + 1)
        absorb(j, s_ref[slot])
        s_ref[1 - slot] = following
        return 0

    lax.fori_loop(0, full, loop, 0)

    def diagonal(size):
        scores = s_ref[full % 2, :size]
        row = lax.broadcasted_iota(jnp.int32, scores.shape, 0)
        column = lax.broadcasted_iota(jnp.int32, scores.shape, 1) % rows
        absorb(full, jnp.where(row + full * block <= column + pos, scores, -1e30))

    half = pos - full * block < block // 2

    @pl.when(half)
    def _():
        diagonal(block // 2)

    @pl.when(jnp.logical_not(half))
    def _():
        diagonal(block)

    total = acc_ref[HD : HD + 1]
    out = acc_ref[:HD] / total
    lse_ref[0, 0] = m_ref[...] + jnp.log(total)
    for g in range(q_ref.shape[3] // PAIR):
        o_ref[0, 0, :, g * PAIR : (g + 1) * PAIR] = back_heads(out, rows, g).astype(BF)


def attend(q, kv, loc, pos):
    pieces, micro, rows, width = q.shape
    count = kv.shape[0]
    stacked = rows * width // HD
    block = min(512, rows * count)
    scores = micro * pieces * stacked * rows * count // 2
    heads = pl.BlockSpec((1, 1, rows, width), lambda m, p, *_: (p, m, 0, 0))
    return call(
        functools.partial(attend_kernel, block),
        [loc, pos, q, kv],
        [shaped(*q.shape), shaped(pieces, micro, 1, stacked, kind=F32)],
        (),
        scores * 2750,
        scores,
        grid_spec=pltpu.PrefetchScalarGridSpec(
            num_scalar_prefetch=2,
            grid=(micro, pieces),
            in_specs=[
                heads,
                pl.BlockSpec((count, 1, rows, PAIR), lambda m, p, *_: (0, m, 0, 0)),
            ],
            out_specs=[
                heads,
                pl.BlockSpec((1, 1, 1, stacked), lambda m, p, *_: (p, m, 0, 0)),
            ],
            scratch_shapes=[
                pltpu.VMEM((count, rows, HD), BF),
                pltpu.VMEM((count, HD + GAIN_ROWS, rows), BF),
                pltpu.VMEM((1, stacked), F32),
                pltpu.VMEM((HD + GAIN_ROWS, stacked), F32),
                pltpu.VMEM((2, block, stacked), F32),
            ],
        ),
    )


def attend_back_kernel(
    block,
    loc_ref,
    pos_ref,
    q_ref,
    do_ref,
    o_ref,
    lse_ref,
    kv_ref,
    cos_ref,
    sin_ref,
    before_ref,
    dq_ref,
    send_ref,
    keep_ref,
    k_ref,
    v_ref,
    kt_ref,
    dq_acc,
    dk_acc,
    dv_acc,
):
    piece = pl.program_id(0)
    rows = q_ref.shape[2]
    count = kv_ref.shape[0]
    per_block = block // rows
    scale = 1.0 / math.sqrt(HD)

    @pl.when(piece == 0)
    def _():
        def one(i, _):
            kv = kv_ref[loc_ref[i], 0]
            k_ref[i] = kv[:, :HD]
            v_ref[i] = kv[:, HD:]
            kt_ref[i] = kv.T[:HD]
            dk_acc[i] = jnp.zeros(dk_acc.shape[1:], F32)
            dv_acc[i] = jnp.zeros(dv_acc.shape[1:], F32)
            return 0

        lax.fori_loop(0, count, one, 0)

    pos = pos_ref[piece]
    q = q_ref[0, 0] * BF(scale)
    do = do_ref[0, 0]
    queries, queries_t = stack_heads(q), turn_heads(q)
    grads, grads_t = stack_heads(do), turn_heads(do)
    dots = turn_heads(do.astype(F32) * o_ref[0, 0].astype(F32))
    delta = jnp.sum(dots, axis=0, keepdims=True)
    logs = lse_ref[0, 0]
    dq_acc[...] = jnp.zeros(dq_acc.shape, F32)

    def step(j, masked, used=per_block):
        first = j * per_block
        keys = jnp.concatenate([k_ref[first + i] for i in range(used)], axis=0)
        values = jnp.concatenate([v_ref[first + i] for i in range(used)], axis=0)
        keys_t = jnp.concatenate([kt_ref[first + i] for i in range(used)], axis=1)
        scores = product(keys, queries_t)
        probs = jnp.exp(scores - logs)
        if masked:
            row = lax.broadcasted_iota(jnp.int32, scores.shape, 0)
            column = lax.broadcasted_iota(jnp.int32, scores.shape, 1) % rows
            probs = jnp.where(row + j * block <= column + pos, probs, 0.0)
        grad_probs = product(values, grads_t)
        grad_low = (probs * (grad_probs - delta)).astype(BF)
        dv = product(probs.astype(BF), grads)
        dk = product(grad_low, queries)
        dq_acc[...] += product(keys_t, grad_low)
        for i in range(used):
            dk_acc[first + i] += dk[i * rows : (i + 1) * rows]
            dv_acc[first + i] += dv[i * rows : (i + 1) * rows]

    full = pos // block

    def loop(j, _):
        step(j, False)
        return 0

    lax.fori_loop(0, full, loop, 0)
    half = pos - full * block < block // 2

    @pl.when(half)
    def _():
        step(full, True, per_block // 2)

    @pl.when(jnp.logical_not(half))
    def _():
        step(full, True)

    first = lax.broadcasted_iota(jnp.int32, (rows, PAIR), 1) % HD < HD // 2
    for g in range(q_ref.shape[3] // PAIR):
        part = back_heads(dq_acc[...], rows, g) * scale
        turned = jnp.where(
            first, pltpu.roll(part, PAIR - HD // 2, 1), pltpu.roll(part, HD // 2, 1)
        )
        out = part * cos_ref[...] - turned * sin_ref[...]
        dq_ref[0, 0, :, g * PAIR : (g + 1) * PAIR] = out.astype(BF)

    @pl.when(piece == pl.num_programs(0) - 1)
    def _():
        pieces = pl.num_programs(0)

        def one(i, _):
            grad = jnp.concatenate([dk_acc[i], dv_acc[i]], axis=1).astype(BF)
            place = loc_ref[i]
            owner = place // pieces
            slot = owner // 2 * pieces + place % pieces

            @pl.when(owner % 2 == 0)
            def _():
                keep_ref[slot] = grad

            @pl.when(owner % 2 == 1)
            def _():
                send_ref[slot] = grad

            return 0

        lax.fori_loop(0, count, one, 0)


def attend_back(m, q, grad, attended, lse, kv, cos, sin, loc, pos, before):
    pieces, micro, rows, width = q.shape
    count = kv.shape[0]
    stacked = rows * width // HD
    block = min(512, rows * count)
    scores = pieces * stacked * rows * count // 2
    heads = pl.BlockSpec((1, 1, rows, width), lambda p, *_: (p, m, 0, 0))
    half = pl.BlockSpec((count // 2, rows, PAIR), lambda p, *_: (0, 0, 0))
    table = pl.BlockSpec((rows, PAIR), lambda p, *_: (p, 0))
    return call(
        functools.partial(attend_back_kernel, block),
        [loc, pos, q, grad, attended, lse, kv, cos, sin, before],
        [shaped(*q.shape)] + [shaped(count // 2, rows, PAIR)] * 2,
        (),
        scores * 4600,
        scores,
        input_output_aliases={9: 0} if m else {},
        grid_spec=pltpu.PrefetchScalarGridSpec(
            num_scalar_prefetch=2,
            grid=(pieces,),
            in_specs=[
                heads,
                heads,
                heads,
                pl.BlockSpec((1, 1, 1, stacked), lambda p, *_: (p, m, 0, 0)),
                pl.BlockSpec((count, 1, rows, PAIR), lambda p, *_: (0, m, 0, 0)),
                table,
                table,
                ANY,
            ],
            out_specs=[heads, half, half],
            scratch_shapes=[
                pltpu.VMEM((count, rows, HD), BF),
                pltpu.VMEM((count, rows, HD), BF),
                pltpu.VMEM((count, HD, rows), BF),
                pltpu.VMEM((HD, stacked), F32),
                pltpu.VMEM((count, rows, HD), F32),
                pltpu.VMEM((count, rows, HD), F32),
            ],
        ),
        light=True,
    )


def rope_tables(positions):
    inverse = 1.0 / 10000.0 ** (jnp.arange(0, HD, 2).astype(F32) / HD)
    angle = positions.astype(F32)[:, None] * inverse[None, :]
    cos, sin = jnp.cos(angle), jnp.sin(angle)
    cos_head = jnp.concatenate([cos, cos], axis=1)
    sin_head = jnp.concatenate([-sin, sin], axis=1)
    ones, zeros = jnp.ones_like(cos_head), jnp.zeros_like(sin_head)
    return (
        jnp.concatenate([cos_head, cos_head], axis=1),
        jnp.concatenate([sin_head, sin_head], axis=1),
        jnp.concatenate([cos_head, ones], axis=1),
        jnp.concatenate([sin_head, zeros], axis=1),
    )


def normalize(values, gain):
    scale = lax.rsqrt(jnp.mean(values * values, axis=-1, keepdims=True) + EPSILON)
    return scale, (values * scale * gain).astype(BF)


def normalize_back(values, scale, gain, grad):
    norm = values * scale
    scaled = grad * gain
    inner = scale * (scaled - norm * jnp.mean(scaled * norm, axis=-1, keepdims=True))
    return inner, jnp.sum(grad * norm, axis=0)


class Sizes:
    def __init__(self, tokens, w_query):
        self.micro, self.held, self.width = tokens.shape
        self.rows = self.held // 2
        self.count = lax.axis_size("wide")
        self.depth = self.width // self.count
        self.heads = w_query.shape[2] // 2
        self.qkv = self.heads + PAIR


def shards(
    tokens, out_grad, attn_gain, w_query, w_key, w_value, w_out, ffn_gain, w_gate, w_up, w_down
):
    s = Sizes(tokens, w_query)
    section = lax.axis_index("section")
    wide = lax.axis_index("wide")
    core = lax.axis_index("tp")
    count, rows = s.count, s.rows
    home = section == 0

    pos = jnp.stack(
        [
            jnp.where((core ^ (p // 2)) == 0, 2 * wide, 2 * count - 1 - 2 * wide) * s.held
            + (section ^ (p % 2)) * rows
            for p in range(4)
        ]
    ).astype(jnp.int32)
    order = jnp.arange(4 * count)
    half_block = order // 2
    odd = half_block % 2
    owner = jnp.where(odd == 0, half_block, 2 * count - 1 - half_block) // 2
    loc = ((owner ^ wide) * 4 + (odd ^ core) * 2 + ((order % 2) ^ section)).astype(jnp.int32)
    positions = (pos[:, None] + jnp.arange(rows)[None, :]).reshape(-1)
    tables = rope_tables(positions)
    place = (tables, loc, pos)

    def halves(array, axis):
        size = array.shape[axis] // 2
        own = lax.dynamic_slice_in_dim(array, section * size, size, axis)
        away = lax.dynamic_slice_in_dim(array, (1 - section) * size, size, axis)
        return own, away

    def pack_attn(parts):
        query, key, value, out = parts
        return jnp.concatenate([query, key, value, out.T], axis=1)

    def both_layers(own, away):
        other = partner(away, "section", 1)
        return jnp.where(home, own, other), jnp.where(home, other, own)

    def take(values):
        part = lax.dynamic_slice_in_dim(values, section * rows, rows, 1)
        return mirror(part).reshape(-1, s.width)

    own_gains = jnp.concatenate([attn_gain, ffn_gain], axis=0)
    own_gains = lax.all_gather(own_gains, "wide", axis=1, tiled=True)
    gains_l = [gains.astype(F32) for gains in both_layers(own_gains, own_gains)]
    attn = [halves(w_query[0], 1), halves(w_key[0], 1), halves(w_value[0], 1), halves(w_out[0], 0)]
    attn_l = both_layers(*[pack_attn([part[i] for part in attn]) for i in range(2)])
    gate_h = halves(w_gate[0], 1)
    gate_l = both_layers(gate_h[0], after(gate_h[1], attn_l[0]))
    u = take(tokens).astype(F32)
    first_scale, low = normalize(u, gains_l[0][0])
    normed = spread(low)
    up_h, down_h = halves(w_up[0], 1), halves(w_down[0], 0)
    up_l = both_layers(up_h[0], after(up_h[1], normed[1]))
    down_l = both_layers(down_h[0].T, after(down_h[1].T, up_l[0]))

    gather_all = lambda x: lax.all_gather(x, "wide", axis=0, tiled=True)
    near = lambda x, *events: partner(after(x, *events), "wide", 1)
    attn_0 = gather_all(attn_l[0])
    gate_0 = gather_line(gate_l[0])
    up_0 = gather_line(up_l[0])
    q0, kv_own = qkv_project(normed, attn_0, tables, s.micro, s.qkv)
    down_0 = gather_line(after(down_l[0], q0))
    kv0 = jnp.concatenate(gather_blocks(kv_own), axis=0)
    attn_1 = gather_all(after(attn_l[1], q0))
    kv0, gate_0 = lax.optimization_barrier((kv0, gate_0))
    attended0, lse0 = attend(q0, kv0, loc, pos)
    gate_0 = (gate_0, near(gate_0))
    gate_1 = gather_line(after(gate_l[1], kv0))
    own, send = contract(
        [after(attended0, gate_0[1]).reshape(-1, s.heads)],
        [(attn_0,)],
        (s.qkv,),
        s.depth,
        s.width,
    )
    up_0 = (up_0, near(up_0, gate_0[1], own))
    upstream = take(after(out_grad, own))
    normed_ffn0, middle0, second_scale0, _ = exchange(
        own, send, u, gains_l[0][1], ident=0
    )
    up_1 = gather_line(after(up_l[1], middle0))
    line_down0 = down_0
    down_0 = (down_0, near(down_0, up_0[1], middle0))
    gate0, up0, hidden0 = gate_up(
        [after(normed_ffn0[0], up_0[1], upstream, line_down0), *normed_ffn0[1:]],
        gate_0,
        up_0,
        s.depth,
    )
    upstream_other = after(partner(after(upstream, up_0[1]), "section", 1), hidden0)
    down_1 = gather_line(after(down_l[1], hidden0))
    gate_1 = (gate_1, near(gate_1, down_0[1]))
    own, send = contract(
        [after(hidden0, upstream_other)], [down_0], (None,), s.depth, s.width
    )
    kept0 = (u, first_scale, normed, q0, kv0, attended0, lse0, middle0, second_scale0)
    kept0 += (normed_ffn0, gate0, up0, hidden0)
    normed, u, first_scale, _ = exchange(
        own, send, middle0, gains_l[1][0], keep_f32=False, ident=1
    )
    out0 = u
    q1, kv_own = qkv_project(
        [after(normed[0], gate_1[1]), *normed[1:]], attn_1, tables, s.micro, s.qkv
    )
    kv1 = jnp.concatenate(gather_blocks(kv_own), axis=0)
    up_1 = (up_1, near(up_1, kv1))
    attended1, lse1 = attend(q1, after(kv1, up_1[0]), loc, pos)
    own, send = contract(
        [after(attended1, up_1[1], down_1).reshape(-1, s.heads)], [(attn_1,)], (s.qkv,), s.depth, s.width
    )
    down_1 = (down_1, near(down_1, up_1[1], own))
    normed_ffn1, middle1, second_scale1, _ = exchange(own, send, u, gains_l[1][1], ident=5)
    grad2 = [upstream, upstream_other]
    grad2 += [partner(after(x, normed_ffn1[0]), "tp", 1) for x in grad2]
    gate1, up1, hidden1 = gate_up(
        [after(normed_ffn1[0], down_1[1]), *normed_ffn1[1:]], gate_1, up_1, s.depth
    )
    kept1 = (u, first_scale, normed, q1, kv1, attended1, lse1, middle1, second_scale1)
    kept1 += (normed_ffn1, gate1, up1, hidden1)
    own1, send1 = contract([hidden1], [down_1], (None,), s.depth, s.width)
    layers = [
        (gains_l[0], attn_0, gate_0, up_0, down_0),
        (gains_l[1], attn_1, gate_1, up_1, down_1),
    ]
    kept = [kept0, kept1]

    def near_sum(keep, got):
        total = (keep.astype(F32) + got.astype(F32)).astype(BF)
        return total.reshape(-1, total.shape[-1])

    reduce_all = lambda x: lax.psum_scatter(x, "wide", scatter_dimension=0, tiled=True)

    def give(value, layer):
        value = value.reshape(s.micro, rows, s.width)
        pair = [mirror(value, 0, (layer,)), mirror(value, 1, (1 - layer,))]
        return jnp.concatenate(pair[::-1] if layer else pair, axis=1)

    grads, terms, gain_terms = [None, None], [None, None], []
    by_piece = lambda table: table.reshape(4, rows, PAIR)
    halved = lambda x: x.reshape(count // 2, 4, rows, PAIR)
    for layer in (1, 0):
        gains, attn, gate_w, up_w, down_w = layers[layer]
        u, first_scale, normed, q, kv, attended, lse, middle, second_scale, normed_ffn = kept[
            layer
        ][:10]
        gate, up, hidden = kept[layer][10:]
        flat = attended.reshape(-1, s.heads)
        if layer:
            grad2 = [after(x, own1) for x in grad2]
            given0 = give(after(out0, own1), 0)
        down_send, down_keep = weight_grad(grad2, [hidden], count)
        down_got = partner(down_send, "wide", 1)
        grad_gate, grad_up = hidden_back(
            [after(x, down_send) for x in grad2], down_w, gate, up, s.depth
        )
        gate_send, gate_keep = weight_grad(normed_ffn, [grad_gate], count)
        up_send, up_keep = weight_grad(
            [after(x, gate_send) for x in normed_ffn], [grad_up], count
        )
        if layer:
            out1 = (middle1 + fold(own1, send1)).astype(BF)
            grad_gate, given0 = lax.optimization_barrier((after(grad_gate, out1), given0))
        own, send = contract(
            [after(grad_gate, up_send), grad_up],
            [gate_w, up_w],
            (None, None),
            s.depth,
            s.width,
        )
        down_near = near_sum(down_keep, after(down_got, own))
        if layer == 0:
            own = after(own, d_attn)
            terms[1][0] = d_attn
        d_down = reduce_line(down_near)
        gate_got = partner(after(gate_send, down_near), "wide", 1)
        grad1, grad_middle, second_gain, _ = exchange(
            after(own, down_near), send, upstream, gains[1], middle, second_scale, ident=2
        )
        gate_got, d_down = after((gate_got, d_down), grad1[0])
        gate_near = near_sum(gate_keep, gate_got)
        d_gate = reduce_line(gate_near)
        up_got = partner(after(up_send, gate_near, d_down), "wide", 1)
        grad1 = [after(grad1[0], gate_near, d_down), *grad1[1:]]
        grad_attended = out_back(grad1, attn, s.qkv, s.heads)
        if layer == 0:
            crossed = [partner_one(x, 0) for x in after(tuple(terms[1]), grad_attended)]
        else:
            given1 = give(after(out1, grad_attended), 1)
        back = lambda m, grad, before: attend_back(
            m, q, grad, attended, lse, kv, tables[0], tables[1], loc, pos, before
        )
        grad_attended = grad_attended.reshape(q.shape)
        dq, send0, keep0 = back(0, grad_attended, q)
        got0 = partner(halved(send0), "wide", 1)
        if layer == 0:
            down_crossed = partner_one(after(d_down, send0), 1)
        dq, send1_, keep1 = back(1, after(grad_attended, send0), dq)
        if layer == 0:
            dq, down_crossed = lax.optimization_barrier((dq, down_crossed))
        up_got, got0, d_gate = after((up_got, got0, d_gate), dq)
        near0 = reduce_near(halved(keep0), got0)
        if layer == 0:
            gate_crossed = partner_one(after(d_gate, near0), 1)
        got1 = partner(after(halved(send1_), near0), "wide", 1)
        dkv0 = reduce_far(near0)
        up_near = near_sum(up_keep, after(up_got, near0))
        d_up = reduce_line(up_near)
        out_send, out_keep = weight_grad(
            [after(x, up_near, d_gate) for x in grad1], [flat], count
        )
        if layer:
            out_send, given1 = lax.optimization_barrier((out_send, given1))
            section_out = jnp.where(home, given0, given1)
        dkv1 = reduce_far(reduce_near(halved(keep1), after(got1, out_send)))
        if layer == 0:
            crossed = list(after(tuple(crossed), dq))
            dkv1 = after(dkv1, *crossed)
        half = HD // 2
        back_rows = []
        for dkv in (dkv0, dkv1):
            turned = jnp.concatenate(
                [dkv[..., half:HD], dkv[..., :half], jnp.zeros_like(dkv[..., HD:])], axis=-1
            )
            back_rows.append(dkv * by_piece(tables[2]) - turned * by_piece(tables[3]))
        dkv = jnp.stack(back_rows, axis=1).astype(BF)
        dq, dkv = after(dq, out_send).reshape(-1, s.heads), dkv.reshape(-1, PAIR)
        if layer == 0:
            out_got = partner(after(out_send, got1), "wide", 1)
            dkv, gate_crossed = lax.optimization_barrier((dkv, gate_crossed))
            crossed_0 = [gate_crossed, down_crossed]
        own, send = contract([dq, dkv], [(attn,), (attn,)], (0, s.heads), s.depth, s.width)
        if layer == 0:
            out_near = near_sum(out_keep, after(out_got, own))
            d_out = reduce_line(out_near)
            own = after(own, out_near)
        qkv_send, qkv_keep = weight_grad(
            [after(x, own) for x in normed], [dq, dkv], count
        )
        if layer:
            pack_got = partner(
                jnp.concatenate([after(qkv_send, dkv1), out_send], axis=2), "wide", 1
            )
            grad2, _, first_gain, _ = exchange(
                after(own, qkv_send),
                send,
                grad_middle,
                gains[0],
                u,
                first_scale,
                keep_f32=False,
                ident=3,
            )
            grads[1] = upstream = grad2[0]
            pack_got, d_up = after((pack_got, d_up), grad2[0])
            pack_near = near_sum(jnp.concatenate([qkv_keep, out_keep], axis=2), pack_got)
            d_attn = reduce_line(after(pack_near, d_up))
            grad2 = [after(x, pack_near) for x in grad2]
            terms[1] = [None, d_gate, d_up, d_down]
        else:
            grads[0], _, first_gain, got = exchange(
                own,
                send,
                grad_middle,
                gains[0],
                u,
                first_scale,
                keep_f32=False,
                last=True,
                bulk=(qkv_send,),
                ident=4,
            )
            grads[0] = grads[0][0]
            qkv_near = near_sum(qkv_keep, got[0])
            grads_out = give(after(grads[1], grads[0]), 1)
            blocks = qkv_near.reshape(count // 2, s.depth, -1)
            d_qkv = blocks[wide // 2].astype(F32)
            for j in range(1, count // 2):
                block = partner(blocks[(wide // 2) ^ j], "wide", 2 * j)
                d_qkv = d_qkv + block.astype(F32)
            d_qkv = d_qkv.astype(BF)
            terms[0] = [d_qkv, d_out, d_gate, d_up, d_down]
        gain_terms += [first_gain.reshape(1, -1), second_gain.reshape(1, -1)]

    given = (give(grads[0], 0), grads_out)
    up_crossed = partner_one(after(d_up, grads[0]), 1)
    d_qkv_out, *given = lax.optimization_barrier((d_qkv, *given))
    input_grads = jnp.where(home, *given)
    late = [partner_one(x, 1) for x in (d_qkv_out, d_out)]
    crossed_0 = [*late, crossed_0[0], up_crossed, crossed_0[1]]
    crossed = [crossed[0][:, : s.qkv], crossed[0][:, s.qkv :], *crossed[1:]]
    terms[1] = [terms[1][0][:, : s.qkv], terms[1][0][:, s.qkv :], *terms[1][1:]]
    gain_total = jnp.concatenate(gain_terms, axis=0)
    gain_total = gain_total + partner(gain_total, "tp", 1)
    gain_total = gain_total + partner(gain_total, "section", 1)
    gain_total = gain_total.reshape(4, count // 2, 2, s.depth)
    gain_total = gain_total[:, :, side()] + partner(gain_total[:, :, 1 - side()], "wide", 1)
    gain_total = after(gain_total, *given)
    total = gain_total[:, wide // 2]
    for j in range(1, count // 2):
        total = total + partner(gain_total[:, (wide // 2) ^ j], "wide", 2 * j)
    gain_total = total
    gains = jnp.where(home, gain_total[2:], gain_total[:2])

    def settle(index):
        own = jnp.where(home, terms[0][index], terms[1][index]).astype(F32)
        other = crossed[index].astype(F32) + crossed_0[index].astype(F32)
        return jnp.where(home, own, other), jnp.where(home, other, own)

    heads = s.heads
    low, high = settle(0)
    cut = lambda start, size: jnp.concatenate(
        [low[:, start : start + size], high[:, start : start + size]], axis=1
    )
    d_query = cut(0, heads)
    d_key = cut(heads, HD)
    d_value = cut(heads + HD, HD)
    d_out = jnp.concatenate([half.T for half in settle(1)], axis=0)
    d_gate = jnp.concatenate(settle(2), axis=1)
    d_up = jnp.concatenate(settle(3), axis=1)
    d_down = jnp.concatenate([half.T for half in settle(4)], axis=0)
    return (
        section_out[None],
        input_grads[None],
        gains[0:1],
        d_query[None],
        d_key[None],
        d_value[None],
        d_out[None],
        gains[1:2],
        d_gate[None],
        d_up[None],
        d_down[None],
    )


def solution(mesh):
    return jax.shard_map(
        shards,
        mesh=mesh,
        in_specs=(
            P(None, ("wide", "tp"), None),
            P(None, ("wide", "tp"), None),
            P("section", "wide"),
            P("section", "wide", "tp"),
            P("section", "wide", "tp"),
            P("section", "wide", "tp"),
            P("section", "tp", "wide"),
            P("section", "wide"),
            P("section", "wide", "tp"),
            P("section", "wide", "tp"),
            P("section", "tp", "wide"),
        ),
        out_specs=(
            P("section", None, ("wide", "tp"), None),
            P("section", None, ("wide", "tp"), None),
            P("section", "wide"),
            P("section", "wide", "tp"),
            P("section", "wide", "tp"),
            P("section", "wide", "tp"),
            P("section", "tp", "wide"),
            P("section", "wide"),
            P("section", "wide", "tp"),
            P("section", "wide", "tp"),
            P("section", "tp", "wide"),
        ),
        check_vma=False,
    )
```
